512 devices in a mesh: section: 4 (over y_lo), expert: 128 (over y_hi, x, z, core).
Axes of the slice: x: 4, y: 8 (y_hi: 2, y_lo: 4; y = y_hi * 4 + y_lo), z: 8, core: 2. Of those that a mesh axis runs over, the one named last changes fastest.
Arguments:
- enc_states: bfloat16 [4, 16384, 2080], P('section', 'expert'), may hold values from -6 to 6
- patch_start: int32 [128], P('expert'), may hold values from 0 to 120
- patch_layer: int32 [128], P('expert'), may hold values from 1 to 3
- enc_gain: float32 [2080], replicated, may hold values from 0.1 to 1.9
- dec_states: bfloat16 [4, 2048, 2080], P('section', 'expert'), may hold values from -6 to 6
- queries: bfloat16 [4, 2048, 1024], P('section', 'expert'), may hold values from -1.796875 to 1.796875
- attn_weight: bfloat16 [4, 3, 2080, 1024], P('section', None, None, 'expert'), may hold values from -0.125 to 0.125
- ffn_gain: float32 [4, 2080], P('section'), may hold values from 0.1 to 1.9
- expert_in: bfloat16 [4, 128, 2080, 384], P('section', 'expert'), may hold values from -0.125 to 0.125
- expert_out: bfloat16 [4, 128, 384, 2080], P('section', 'expert'), may hold values from -0.109375 to 0.109375
- expert_id: int32 [4, 2048, 1], P('section', 'expert'), may hold values from 0 to 15; in each aligned block of 16 rows (0 to 15, 16 to 31, ..., all dimensions but the last counted through in order) at most 2 rows name the same one
- gate: float32 [4, 2048], P('section', 'expert'), may hold values from 0.3 to 1
Outputs:
- layer_out: bfloat16 [4, 2048, 2080], P('section', 'expert')
- memory: bfloat16 [16384, 2080], P('expert')
The draws below stay inside these ranges and needn't reach their ends.
Inputs may be any that keep to these rules, and one draw needn't show every extreme that they name: `expert_id`: within the 16 rows of one device of each section no expert is named more than 2 times, and some device's rows name one expert exactly 2 times.
All inputs are finite; a program needn't handle non-finite values.
Results may differ from the reference program's by a relative error of at most 0.017.
Values may be sent and summed in bfloat16 or wider, within the bound.
A program may use at most 128 MiB of HBM per device.

```python
import math
import jax
import jax.numpy as jnp
import numpy as np
from jax import lax

D = 2080
HEAD_DIM = 64
HEADS = 16
FF_WIN = 3072
SPLIT = 8
PATCH = 8
SRC_LEN = 128
TGT_LEN = 16
CAP = 2
MEMORY_ROWS_TOTAL = 16384
TOK_ALL = 2048
N_SECTION = 4
N_EXPERT = 128


def touch_ends(drawn, key, least, high):
    longest = drawn.shape.index(max(drawn.shape))
    spots = []
    for shift in (0, 1):
        where = [jax.random.randint(jax.random.fold_in(key, axis), (), 0, length) for axis, length in enumerate(drawn.shape)]
        where[longest] = (where[longest] + shift) % drawn.shape[longest]
        spots.append(tuple(where))
    return drawn.at[spots[0]].set(least).at[spots[1]].set(high)


def block_scale(key, dims, shards, smallest, top_value):
    def one(dim, parts):
        steps = jax.random.uniform(jax.random.fold_in(jax.random.fold_in(key, 6), dim), (parts,), jnp.float32, smallest / len(shards), top_value / len(shards))
        return jnp.repeat(jnp.exp(steps), dims[dim] // parts).reshape((-1,) + (1,) * (len(dims) - dim - 1))

    factor_of = one(*shards[0])
    for cut in shards[1:]:
        factor_of = factor_of * one(*cut)
    return factor_of


def assign_block(own_key, own, number, rows, number_of, top, reach, slope):
    ranking = jax.random.permutation(own_key, number_of)
    crowded, ordinary = portions_of(number_of, rows * top, reach, slope, True), portions_of(number_of, rows * top, reach, slope, False)
    places = jnp.arange(number_of)

    def named(tallies, offset_by):
        used = int((tallies > 0).sum())
        fixed = max(1, used // 4)
        shifted = fixed + (places - fixed + offset_by * (used - fixed)) % max(1, number_of - fixed)
        return jnp.zeros((number_of,), jnp.int32).at[ranking[jnp.where(places < fixed, places, shifted)]].set(jnp.asarray(tallies, jnp.int32))

    tallies = jnp.where(number % 4 == 0, named(crowded, number // 4), named(ordinary, number - number // 4 - 1))
    mixed = jax.random.permutation(jax.random.fold_in(own, 3), number_of)
    donor, sink = mixed[0:number_of // 2 * 2:2], mixed[1:number_of // 2 * 2:2]
    room = jnp.minimum(tallies[donor] - 1, reach - tallies[sink]) // 2
    room = jnp.where((donor == ranking[0]) | (sink == ranking[0]) | (tallies[sink] == 0), 0, jnp.maximum(room, 0))
    shifted = jax.random.randint(jax.random.fold_in(own, 4), (number_of // 2,), 0, 1 << 20) % (room + 1)
    tallies = tallies.at[donor].add(-shifted).at[sink].add(shifted)
    items = jnp.searchsorted(jnp.cumsum(tallies), jnp.arange(rows * top), side="right").astype(jnp.int32)
    grid = items.reshape(top, rows).T
    grid = grid[jax.random.permutation(jax.random.fold_in(own, 1), rows)]
    offset_by = jax.random.randint(jax.random.fold_in(own, 2), (rows, 1), 0, top)
    return jnp.take_along_axis(grid, (jnp.arange(top)[None, :] + offset_by) % top, axis=1)


def portions_of(count, total, most, lean, full):
    weights = [(1 << 20) // math.isqrt(grade ** lean) + 1 for grade in range(1, count + 1)]
    largest = most if full else min(most, max(-(-total // count), total * weights[0] // sum(weights)))
    least = 1 if total - largest >= count - 1 else 0
    counts, spare = [largest] + [least] * (count - 1), total - largest - least * (count - 1)
    while spare > 0:
        free = [i for i in range(1, count) if counts[i] < largest] or [i for i in range(1, count) if counts[i] < most]
        pool, remaining = sum([weights[i] for i in free]), spare
        for i in free:
            extra = min(most - counts[i], max(1, remaining * weights[i] // pool), spare)
            counts[i] = counts[i] + extra
            spare = spare - extra
    return np.array(counts)


def normal_values(own_key, dims, deviation, limit, cuts=(), held_as=jnp.bfloat16):
    result = jax.random.normal(own_key, dims, jnp.float32) * deviation
    if len(cuts) > 0:
        result = block_scale(own_key, dims, cuts, -0.22, 0.18) * result
    return jnp.clip(result, min=-limit, max=limit).astype(held_as)


def setup_inputs(seed: int = 0) -> dict:
    streams_of = jax.random.split(jax.random.key(seed), 13)
    enc_states = normal_values(streams_of[0], (N_SECTION, MEMORY_ROWS_TOTAL, D), 1.0, 6.0, ((0, 4), (1, 128)))
    patch_start = touch_ends(jax.random.randint(streams_of[1], (N_EXPERT,), 0, SRC_LEN - PATCH + 1), jax.random.fold_in(streams_of[1], 1), 0, SRC_LEN - PATCH).astype(jnp.int32)
    patch_layer = touch_ends(jax.random.randint(streams_of[2], (N_EXPERT,), 1, N_SECTION), jax.random.fold_in(streams_of[2], 1), 1, N_SECTION - 1).astype(jnp.int32)
    enc_gain = jnp.clip(1.0 + 0.18 * jax.random.normal(streams_of[3], (D,), jnp.float32), 0.1, 1.9)
    dec_states = normal_values(streams_of[4], (N_SECTION, TOK_ALL, D), 1.0, 6.0, ((0, 4), (1, 128)))
    queries = normal_values(streams_of[5], (N_SECTION, TOK_ALL, HEADS * HEAD_DIM), 0.3, 1.796875, ((0, 4), (1, 128)))
    attn_weight = normal_values(streams_of[6], (N_SECTION, 3, D, HEADS * HEAD_DIM), D ** -0.5, 0.125, ((0, 4), (3, 128)))
    ffn_gain = jnp.clip(1.0 + 0.18 * jax.random.normal(streams_of[7], (N_SECTION, D), jnp.float32), 0.1, 1.9)
    expert_in = normal_values(streams_of[8], (N_SECTION, N_EXPERT, D, FF_WIN // SPLIT), D ** -0.5, 0.125, ((0, 4), (1, 128)))
    expert_out = normal_values(streams_of[9], (N_SECTION, N_EXPERT, FF_WIN // SPLIT, D), FF_WIN ** -0.5, 0.109375, ((0, 4), (1, 128)))
    expert_id_keys = jax.random.split(jax.random.fold_in(streams_of[10], 1), N_SECTION * TOK_ALL // TGT_LEN)
    expert_id_turns = jax.random.permutation(jax.random.fold_in(streams_of[10], 3), N_SECTION * TOK_ALL // TGT_LEN)
    expert_id = jax.vmap(lambda own, number: assign_block(jax.random.fold_in(streams_of[10], 2), own, number, TGT_LEN, N_EXPERT // SPLIT, 1, CAP, 2))(expert_id_keys, expert_id_turns).reshape((N_SECTION, TOK_ALL, 1))
    gate = jnp.clip(0.3 + 0.7 * jax.random.uniform(streams_of[11], (N_SECTION, TOK_ALL), jnp.float32) ** block_scale(streams_of[11], (N_SECTION, TOK_ALL), ((0, 4), (1, 128)), -0.2, 0.2), 0.3, 1.0)
    return dict(enc_states=enc_states, patch_start=patch_start, patch_layer=patch_layer, enc_gain=enc_gain, dec_states=dec_states, queries=queries, attn_weight=attn_weight, ffn_gain=ffn_gain, expert_in=expert_in, expert_out=expert_out, expert_id=expert_id, gate=gate)


def rms_norm(values, gain):
    return values * lax.rsqrt(lax.optimization_barrier(jnp.mean(values * values, axis=-1, keepdims=True)) + 1e-06) * gain

def reference(enc_states, patch_start, patch_layer, enc_gain, dec_states, queries, attn_weight, ffn_gain, expert_in, expert_out, expert_id, gate):
    experts = N_EXPERT // SPLIT
    capacity = min(TGT_LEN, max(2, 2 * TGT_LEN // experts))
    ff_part = FF_WIN // SPLIT
    inner_width = HEADS * HEAD_DIM
    states = enc_states.reshape(N_SECTION, N_EXPERT, SRC_LEN, D)
    positions = jnp.arange(SRC_LEN, dtype=jnp.int32)
    in_window = (positions[None, :] >= patch_start[:, None]) & (positions[None, :] < patch_start[:, None] + PATCH)
    patched = states[0]
    for section_at in range(1, N_SECTION):
        picked = in_window & (patch_layer[:, None] == section_at)
        patched = jnp.where(picked[:, :, None], states[section_at], patched)
    memory = rms_norm(patched.astype(jnp.float32), enc_gain).astype(jnp.bfloat16)
    memory_flat = memory.reshape(N_EXPERT * SRC_LEN, D)
    expert_range = jnp.arange(experts, dtype=jnp.int32)
    slot_range = jnp.arange(capacity, dtype=jnp.int32)
    outputs = []
    for section_at in range(N_SECTION):
        weights = attn_weight[section_at]
        key_matrix_rows = jnp.dot(memory_flat, weights[0], preferred_element_type=jnp.float32).reshape(N_EXPERT, SRC_LEN, HEADS, HEAD_DIM)
        value_matrix_rows = jnp.dot(memory_flat, weights[1], preferred_element_type=jnp.float32).reshape(N_EXPERT, SRC_LEN, HEADS, HEAD_DIM)
        query_matrix_rows = queries[section_at].astype(jnp.float32).reshape(N_EXPERT, TGT_LEN, HEADS, HEAD_DIM)
        logit_scores = jnp.einsum('nthd,nmhd->nhtm', query_matrix_rows, key_matrix_rows)
        exponent = jnp.exp(logit_scores)
        device_portions = exponent / lax.optimization_barrier(jnp.sum(exponent, axis=-1, keepdims=True))
        context = jnp.einsum('nhtm,nmhd->nthd', device_portions, value_matrix_rows).reshape(N_EXPERT * TGT_LEN, inner_width).astype(jnp.bfloat16)
        attended = jnp.dot(context, weights[2].T, preferred_element_type=jnp.float32)
        residual = (dec_states[section_at].astype(jnp.float32) + attended).astype(jnp.bfloat16)
        normed = rms_norm(residual.astype(jnp.float32), ffn_gain[section_at]).astype(jnp.bfloat16)
        expert_ids = expert_id[section_at, :, 0].reshape(N_EXPERT, TGT_LEN)
        member = (expert_ids[:, :, None] == expert_range[None, None, :]).astype(jnp.int32)
        earlier = jnp.cumsum(member, axis=1)
        slot_index = lax.optimization_barrier(jnp.sum(member * earlier, axis=2)) - 1
        select_map = ((expert_ids[:, None, None, :] == expert_range[None, :, None, None]) & (slot_index[:, None, None, :] == slot_range[None, None, :, None])).astype(jnp.float32)
        dispatch = jnp.einsum('nect,ntd->necd', select_map, normed.reshape(N_EXPERT, TGT_LEN, D).astype(jnp.float32)).astype(jnp.bfloat16)
        w_in = expert_in[section_at].reshape(experts, SPLIT, D, ff_part)
        w_out = expert_out[section_at].reshape(experts, SPLIT, ff_part, D)

        def expert_apply(operands):
            arrived, in_parts, output_pieces = operands
            token_rows = arrived.reshape(N_EXPERT * capacity, D)
            full_in = jnp.transpose(in_parts, (1, 0, 2)).reshape(D, SPLIT * ff_part)
            hidden = jax.nn.relu(jnp.dot(token_rows, full_in, preferred_element_type=jnp.float32)).astype(jnp.bfloat16)
            hidden_parts = hidden.reshape(N_EXPERT * capacity, SPLIT, ff_part).astype(jnp.float32)
            partial_value = jnp.einsum('rjf,jfd->rjd', hidden_parts, output_pieces.astype(jnp.float32)).astype(jnp.bfloat16)
            return lax.optimization_barrier(jnp.sum(partial_value.astype(jnp.float32), axis=1))
        combined = lax.map(expert_apply, (jnp.transpose(dispatch, (1, 0, 2, 3)), w_in, w_out))
        combined = combined.reshape(experts, N_EXPERT, capacity, D)
        expert_sum = jnp.einsum('nect,encd->ntd', select_map, combined).reshape(N_EXPERT * TGT_LEN, D)
        layer_out = (residual.astype(jnp.float32) + gate[section_at][:, None] * expert_sum).astype(jnp.bfloat16)
        outputs.append(layer_out)
    return (jnp.stack(outputs), memory_flat)
```

```python
import jax
import jax.numpy as jnp
from jax import lax
from jax.experimental import pallas as pl
from jax.experimental.pallas import tpu as pltpu
from jax.sharding import PartitionSpec as P

HEAD_DIM = 64
PATCH = 8
CHUNK = 16
EPS = 1e-06
BF, F32 = jnp.bfloat16, jnp.float32
NT = (((1,), (1,)), ((), ()))
NN = (((1,), (0,)), ((), ()))


def dot(a, b, dims=NN):
    return lax.dot_general(a, b, dims, preferred_element_type=F32)


def kernel(
    start_ref, layer_ref, enc_ref, enc_gain_ref, dec_ref, q_ref, w_ref, ffn_gain_ref,
    w_in_ref, w_out_ref, id_row_ref, id_col_ref, gate_ref,
    out_ref, memory_ref,
    raw, win, mem, w0, wz, qg, part, pr, ds, dbuf, d1, g, y, rb, rz, rt, d2, ret, w_in, w_out,
    load_sem, wx_s, wx_r, raw_s, raw_r, win_s, win_r, q_s, q_r, self_sem,
    xr_s, xr_r, xl_s, xl_r, x2_s, x2_r, sib_s, sib_r, zr_s, zr_r, zl_s, zl_r,
    p_s, p_r, d1_s, d1_r, g_s, g_r, gs_s, gs_r, rb_s, rb_r, rz_s, rz_r, d2_s, d2_r,
):
    s = lax.axis_index("section")
    e = lax.axis_index("expert")
    c = lax.rem(e, 2)
    z = lax.rem(e // 2, 8)
    x = lax.rem(e // 16, 4)
    yh = e // 64
    zh, zl = z // 4, lax.rem(z, 4)

    def at(yy, xx, zz, cc, ss=None):
        return (s if ss is None else ss, ((yy * 4 + xx) * 8 + zz) * 2 + cc)

    def mod(v, n):
        return lax.rem(v + n, n)

    sibling = at(yh, x, z, 1 - c)
    right, left = at(yh, mod(x + 1, 4), z, c), at(yh, mod(x - 1, 4), z, c)
    up, down = at(yh, x, mod(z + 1, 8), c), at(yh, x, mod(z - 1, 8), c)
    me8 = x * 2 + c
    me16 = yh * 8 + x * 2 + zh
    role = [(dx, dc) for dx in range(4) for dc in range(2)]

    def role_of(dx, dc):
        xx = mod(x + dx, 4)
        cc = lax.rem(c + dc, 2)
        return xx, cc

    def expert_of(i):
        yy = lax.rem(yh + i // 8, 2)
        xx = mod(x + (i // 2) % 4, 4)
        if i % 2:
            zz_h, zz_l = 1 - zh, 3 - zl
        else:
            zz_h, zz_l = zh, zl
        return yy * 8 + xx * 2 + zz_h, at(yy, xx, zz_h * 4 + zz_l, c)

    pending = []

    def copy(src, dst, ssem, rsem, dev):
        return pltpu.make_async_remote_copy(
            src_ref=src, dst_ref=dst, send_sem=ssem, recv_sem=rsem, device_id=dev,
            device_id_type=pl.DeviceIdType.MESH,
        )

    def send(src, dst, ssem, rsem, dev):
        d = copy(src, dst, ssem, rsem, dev)
        d.start()
        pending.append(d)

    def arrived(dst, rsem):
        copy(dst, dst, rsem, rsem, sibling).wait_recv()

    loads = [
        pltpu.make_async_copy(w_in_ref, w_in, load_sem.at[0]),
        pltpu.make_async_copy(w_out_ref, w_out, load_sem.at[1]),
    ]
    for d in loads:
        d.start()

    barrier = pltpu.get_barrier_semaphore()
    peers = [at(yh, x, z, c, lax.rem(s + k, 4)) for k in (1, 2, 3)]
    peers += [at(yh, *role_of(dx, dc)[:1], z, role_of(dx, dc)[1]) for dx, dc in role[1:]]
    peers += [up, down]
    peers += [at(1 - yh, x, z, cc) for cc in (0, 1)]
    peers += [at(yh, x, zh * 4 + lax.rem(zl + k, 4), c) for k in (1, 2, 3)]
    peers += [expert_of(i)[1] for i in range(1, 16)]
    for dev in peers:
        pl.semaphore_signal(barrier, inc=1, device_id=dev, device_id_type=pl.DeviceIdType.MESH)

    start = start_ref[0]
    layer = layer_ref[0]

    @pl.when(s == 0)
    def _():
        raw[...] = enc_ref[...]

    @pl.when(s > 0)
    def _():
        row = lax.broadcasted_iota(jnp.int32, (16, 128), 0)
        col = lax.broadcasted_iota(jnp.int32, (16, 128), 1)
        pick = ((col == row + start) & (row < PATCH)).astype(F32).astype(BF)
        block = enc_ref[...].reshape(128, enc_ref.shape[-1])
        win[s - 1] = dot(pick, block).astype(BF)

    pl.semaphore_wait(barrier, len(peers))

    for yy in (0, 1):
        here = (yh == yy) & (c == yh)

        @pl.when(here)
        def _(yy=yy):
            pltpu.make_async_copy(w_ref, w0.at[c], self_sem.at[0]).start()

        @pl.when(jnp.logical_not(here))
        def _(yy=yy):
            copy(w_ref, w0.at[c], wx_s.at[yy], wx_r.at[c], at(yy, x, z, yh)).start()

    @pl.when(s == 0)
    def _():
        for k in range(8):
            copy(raw.at[k], raw.at[k], raw_s.at[k], raw_r.at[k], at(yh, x, z, c, 1)).start()

    @pl.when(s > 0)
    def _():
        for k in (1, 2, 3):
            copy(
                win.at[s - 1], win.at[s - 1], win_s.at[k - 1], win_r.at[s - 1],
                at(yh, x, z, c, lax.rem(s + k, 4)),
            ).start()

    for i, (dx, dc) in enumerate(role):
        xx, cc = role_of(dx, dc)
        cols = pl.ds(pl.multiple_of((cc * 4 + xx) * 128, 128), 128)
        if i == 0:
            qg[me8] = q_ref[:, cols]
        else:
            send(q_ref.at[:, cols], qg.at[me8], q_s.at[i], q_r.at[i], at(yh, xx, z, cc))

    def patched_chunk(k):
        @pl.when(s > 0)
        def _():
            arrived(raw.at[k], raw_r.at[k])

        @pl.when((s > 0) & (s < 3))
        def _():
            copy(raw.at[k], raw.at[k], raw_s.at[k], raw_r.at[k], at(yh, x, z, c, s + 1)).start()

        if k == 0:
            for i in range(3):
                @pl.when(s != i + 1)
                def _(i=i):
                    arrived(win.at[i], win_r.at[i])

        row = lax.broadcasted_iota(jnp.int32, (CHUNK, 16), 0) + k * CHUNK - start
        slot = lax.broadcasted_iota(jnp.int32, (CHUNK, 16), 1)
        pick = ((row == slot) & (slot < PATCH)).astype(F32).astype(BF)
        window = jnp.where(layer == 1, win[0], jnp.where(layer == 2, win[1], win[2]))
        fresh = dot(pick, window)
        at_row = lax.broadcasted_iota(jnp.int32, fresh.shape, 0) + k * CHUNK - start
        values = jnp.where((at_row >= 0) & (at_row < PATCH), fresh, raw[k].astype(F32))
        scale = lax.rsqrt(jnp.mean(values * values, axis=-1, keepdims=True) + EPS)
        normed = (values * scale * enc_gain_ref[...]).astype(BF)
        mem[me8, k] = normed
        memory_ref[k] = normed
        send(mem.at[me8, k], mem.at[me8, k], xr_s.at[k], xr_r.at[k], right)
        send(mem.at[me8, k], mem.at[me8, k], xl_s.at[k], xl_r.at[k], left)
        send(mem.at[me8, k], mem.at[me8, k], sib_s.at[0, k], sib_r.at[0, k], sibling)

    q_left, q_right, q_far = (mod(x + d, 4) * 2 + c for d in (3, 1, 2))

    def neighbour_chunk(k):
        arrived(mem.at[q_left, k], xr_r.at[k])
        block = mem.at[q_left, k]
        if k < 4:
            send(block, block, x2_s.at[k], x2_r.at[k], right)
        send(block, block, sib_s.at[3, k], sib_r.at[3, k], sibling)
        arrived(mem.at[q_right, k], xl_r.at[k])
        block = mem.at[q_right, k]
        if k >= 4:
            send(block, block, x2_s.at[k], x2_r.at[k], left)
        send(block, block, sib_s.at[1, k], sib_r.at[1, k], sibling)

    def far_chunk(k):
        block = mem.at[q_far, k]
        arrived(block, x2_r.at[k])
        send(block, block, sib_s.at[2, k], sib_r.at[2, k], sibling)

    def own_weights():
        for cc in (0, 1):
            here = (c == yh) & (c == cc)

            @pl.when(here)
            def _(cc=cc):
                pltpu.make_async_copy(w_ref, w0.at[cc], self_sem.at[0]).wait()

            @pl.when(jnp.logical_not(here))
            def _(cc=cc):
                arrived(w0.at[cc], wx_r.at[cc])

        for m in range(3):
            both = jnp.concatenate([w0[0, m].astype(F32), w0[1, m].astype(F32)], axis=0)
            wz[m, z] = both.astype(BF)
        ring_step(1)

    def ring_blocks(r):
        if r < 4:
            return pl.ds(0, 3), pl.ds(0, 3)
        return pl.ds(0, 2), pl.ds(2, 1)

    def ring_step(r):
        ms_up, ms_down = ring_blocks(r)
        block = wz.at[ms_up, mod(z - (r - 1), 8)]
        send(block, block, zr_s.at[r - 1], zr_r.at[r - 1], up)
        block = wz.at[ms_down, mod(z + (r - 1), 8)]
        send(block, block, zl_s.at[r - 1], zl_r.at[r - 1], down)

    def ring_arrived(r):
        ms_up, ms_down = ring_blocks(r)
        arrived(wz.at[ms_up, mod(z - r, 8)], zr_r.at[r - 1])
        arrived(wz.at[ms_down, mod(z + r, 8)], zl_r.at[r - 1])
        if r < 4:
            ring_step(r + 1)

    A, B, C, Z = patched_chunk, neighbour_chunk, far_chunk, ring_arrived
    A(0), A(1), own_weights(), A(2), A(3), B(0), Z(1), A(4), B(1), A(5), B(2), A(6), Z(2), B(3)
    A(7), B(4), B(5), Z(3), B(6), B(7), C(0), C(1), C(2), C(3), Z(4), C(4), C(5), C(6), C(7)
    for dx in range(4):
        q = mod(x + dx, 4) * 2 + (1 - c)
        for k in range(8):
            arrived(mem.at[q, k], sib_r.at[dx, k])
    for i, (dx, dc) in enumerate(role[1:], 1):
        arrived(qg.at[mod(x - dx, 4) * 2 + lax.rem(c + dc, 2)], q_r.at[i])

    width = enc_ref.shape[-1]
    first_head = lax.broadcasted_iota(jnp.int32, (16, 128), 1) < HEAD_DIM

    def attend(q, carry):
        rows = mem[q].reshape(128, width)
        kv = dot(rows, wz[0:2].reshape(256, width), NT)
        keys, values = kv[:, :128].astype(BF), kv[:, 128:].astype(BF)
        ask = qg[q].astype(F32)
        ask = jnp.concatenate([jnp.where(first_head, ask, 0.0), jnp.where(first_head, 0.0, ask)], axis=0)
        exponent = jnp.exp(dot(ask.astype(BF), keys, NT))
        shares = exponent / jnp.sum(exponent, axis=-1, keepdims=True)
        mixed = dot(shares.astype(BF), values)
        context = jnp.where(first_head, mixed[:16], mixed[16:]).astype(BF)
        part[q] = dot(context, wz[2].reshape(128, width)).astype(BF)
        return carry

    lax.fori_loop(0, 8, attend, 0)

    for i, (dx, dc) in enumerate(role[1:], 1):
        xx, cc = role_of(dx, dc)
        send(part.at[xx * 2 + cc], pr.at[me8], p_s.at[i], p_r.at[i], at(yh, xx, z, cc))
    total = dec_ref[...].astype(F32) + part[me8].astype(F32)
    for i, (dx, dc) in enumerate(role[1:], 1):
        q = mod(x - dx, 4) * 2 + lax.rem(c + dc, 2)
        arrived(pr.at[q], p_r.at[i])
        total = total + pr[q].astype(F32)
    residual = total.astype(BF)
    total = residual.astype(F32)
    scale = lax.rsqrt(jnp.mean(total * total, axis=-1, keepdims=True) + EPS)
    normed = (total * scale * ffn_gain_ref[...]).astype(BF)

    row = lax.broadcasted_iota(jnp.int32, (16, 16), 0)
    col = lax.broadcasted_iota(jnp.int32, (16, 16), 1)
    id_row, id_col = id_row_ref[...], id_col_ref[...]
    same = (jnp.broadcast_to(id_row, (16, 16)) == jnp.broadcast_to(id_col, (16, 16))).astype(F32)
    slot_row = jnp.sum(jnp.where(row < col, same, 0.0), axis=0, keepdims=True)
    slot_col = jnp.sum(jnp.where(col < row, same, 0.0), axis=1, keepdims=True)
    number = lax.broadcasted_iota(jnp.int32, (32, 16), 0)
    chosen = (lax.rem(number, 16) == id_row) & ((number // 16).astype(F32) == slot_row)
    picked = dot(chosen.astype(F32).astype(BF), normed)
    ds[:, 0, :] = picked[:16]
    ds[:, 1, :] = picked[16:]
    dbuf[...] = ds[...].astype(BF)

    for i in range(1, 16):
        block, dev = expert_of(i)
        send(dbuf.at[block], d1.at[me16], d1_s.at[i], d1_r.at[i], dev)
    d1[me16] = dbuf[me16]

    def back(i):
        yy = lax.rem(yh + i // 8, 2)
        xx = mod(x - (i // 2) % 4, 4)
        return yy * 8 + xx * 2 + (1 - zh if i % 2 else zh)

    for i in range(1, 16):
        arrived(d1.at[back(i)], d1_r.at[i])
    ds[...] = d1[...].astype(F32)
    g[zl, c] = jnp.concatenate([ds[:, 0, :], ds[:, 1, :]], axis=0).astype(BF)

    block = g.at[zl, c]
    for k in (1, 2, 3):
        send(block, block, g_s.at[k], g_r.at[k], at(yh, x, zh * 4 + lax.rem(zl + k, 4), c))
    send(block, block, gs_s.at[0], gs_r.at[0], sibling)
    for d in loads:
        d.wait()
    for k in (1, 2, 3):
        block = g.at[mod(zl - k, 4), c]
        arrived(block, g_r.at[k])
        send(block, block, gs_s.at[k], gs_r.at[k], sibling)
    for k in range(4):
        arrived(g.at[mod(zl - k, 4), 1 - c], gs_r.at[k])

    hidden = jnp.maximum(dot(g[...].reshape(256, width), w_in[...]), 0.0).astype(BF)
    y[...] = dot(hidden, w_out[...], NT).astype(BF).reshape(y.shape)

    order = (1, 2, 3, 0)
    for k in order:
        to = lax.rem(zl + k, 4)
        send(y.at[to, 1 - c], rb.at[to], rb_s.at[k], rb_r.at[k], sibling)
    for k in order:
        to = lax.rem(zl + k, 4)
        arrived(rb.at[to], rb_r.at[k])
        pair = y[to, c].astype(F32) + rb[to].astype(F32)
        if k:
            rt[to] = pair.astype(BF)
            send(rt.at[to], rz.at[zl], rz_s.at[k], rz_r.at[k], at(yh, x, zh * 4 + to, c))
        else:
            total = pair
    for k in (1, 2, 3):
        src = mod(zl - k, 4)
        arrived(rz.at[src], rz_r.at[k])
        total = total + rz[src].astype(F32)
    ds[:, 0, :] = total[:16]
    ds[:, 1, :] = total[16:]
    d2[...] = ds[...].astype(BF)
    for i in range(1, 16):
        block, dev = expert_of(i)
        send(d2.at[block], ret.at[me16], d2_s.at[i], d2_r.at[i], dev)
    ret[me16] = d2[me16]
    for i in range(1, 16):
        arrived(ret.at[back(i)], d2_r.at[i])
    ds[...] = ret[...].astype(F32)
    slots = jnp.concatenate([ds[:, 0, :], ds[:, 1, :]], axis=0).astype(BF)
    number = lax.broadcasted_iota(jnp.int32, (16, 32), 1)
    chosen = (lax.rem(number, 16) == id_col) & ((number // 16).astype(F32) == slot_col)
    combined = dot(chosen.astype(F32).astype(BF), slots)
    out_ref[...] = (residual.astype(F32) + gate_ref[...] * combined).astype(BF)

    for d in pending:
        d.wait_send()
    for yy in (0, 1):
        @pl.when(jnp.logical_not((yh == yy) & (c == yh)))
        def _(yy=yy):
            copy(w_ref, w0.at[c], wx_s.at[yy], wx_r.at[c], at(yy, x, z, yh)).wait_send()

    @pl.when(s < 3)
    def _():
        for k in range(8):
            copy(raw.at[k], raw.at[k], raw_s.at[k], raw_r.at[k], sibling).wait_send()

    @pl.when(s > 0)
    def _():
        for k in (1, 2, 3):
            copy(
                win.at[s - 1], win.at[s - 1], win_s.at[k - 1], win_r.at[s - 1], sibling
            ).wait_send()


def per_device(
    enc_states, patch_start, patch_layer, enc_gain, dec_states, queries, attn_weight, ffn_gain,
    expert_in, expert_out, expert_id, gate,
):
    rows, width = enc_states.shape[1:]
    hid = expert_in.shape[-1]
    dma = lambda *shape: pltpu.SemaphoreType.DMA(shape)
    vm = lambda *shape: pltpu.VMEM(shape, BF)
    vmem = pl.BlockSpec(memory_space=pltpu.VMEM)
    smem = pl.BlockSpec(memory_space=pltpu.SMEM)
    hbm = pl.BlockSpec(memory_space=pl.ANY)
    scratch = [
        vm(8, 16, width), vm(3, 16, width), vm(8, 8, 16, width), vm(2, 3, 8, width),
        vm(3, 8, 16, width), vm(8, 16, 128), vm(8, 16, width), vm(8, 16, width),
        pltpu.VMEM((16, 2, width), F32), vm(16, 2, width), vm(16, 2, width),
        vm(4, 2, 32, width), vm(4, 2, 32, width), vm(4, 32, width), vm(4, 32, width),
        vm(4, 32, width), vm(16, 2, width), vm(16, 2, width), vm(width, hid), vm(width, hid),
        dma(2), dma(2), dma(2), dma(8), dma(8), dma(3), dma(3), dma(8), dma(8), dma(1),
        dma(8), dma(8), dma(8), dma(8), dma(8), dma(8), dma(4, 8), dma(4, 8),
        dma(4), dma(4), dma(4), dma(4),
        dma(8), dma(8), dma(16), dma(16), dma(4), dma(4), dma(4), dma(4), dma(4), dma(4),
        dma(4), dma(4), dma(16), dma(16),
    ]
    out, memory = pl.pallas_call(
        kernel,
        out_shape=(
            jax.ShapeDtypeStruct(dec_states.shape[1:], BF),
            jax.ShapeDtypeStruct((8, 16, width), BF),
        ),
        in_specs=[smem, smem] + [vmem] * 6 + [hbm, hbm] + [vmem] * 3,
        out_specs=(vmem, vmem),
        scratch_shapes=scratch,
        compiler_params=pltpu.CompilerParams(
            collective_id=0, has_side_effects=True, vmem_limit_bytes=50 * 1024 * 1024
        ),
    )(
        patch_start, patch_layer, enc_states[0].reshape(8, 16, width), enc_gain.reshape(1, width),
        dec_states[0], queries[0], jnp.transpose(attn_weight[0], (0, 2, 1)), ffn_gain,
        expert_in[0, 0], expert_out[0, 0].T, expert_id[0].reshape(1, 16), expert_id[0],
        gate.reshape(16, 1),
    )
    return out[None], memory.reshape(rows, width)


def solution(mesh):
    in_specs = (
        P("section", "expert", None),
        P("expert"),
        P("expert"),
        P(),
        P("section", "expert", None),
        P("section", "expert", None),
        P("section", None, None, "expert"),
        P("section", None),
        P("section", "expert", None, None),
        P("section", "expert", None, None),
        P("section", "expert", None),
        P("section", "expert"),
    )
    out_specs = (P("section", "expert", None), P("expert", None))
    return jax.shard_map(
        per_device, mesh=mesh, in_specs=in_specs, out_specs=out_specs, check_vma=False
    )
```

```python
import jax
import jax.numpy as jnp
from jax import lax
from jax.experimental import pallas as pl
from jax.experimental.pallas import tpu as pltpu
from jax.sharding import PartitionSpec as P

HEAD_DIM = 64
PATCH = 8
CHUNK = 16
EPS = 1e-06
BF, F32 = jnp.bfloat16, jnp.float32
NT = (((1,), (1,)), ((), ()))
NN = (((1,), (0,)), ((), ()))


def dot(a, b, dims=NN):
    return lax.dot_general(a, b, dims, preferred_element_type=F32)


def kernel(
    start_hbm, layer_hbm, enc_hbm, enc_gain_hbm, dec_hbm, q_hbm, w_hbm, ffn_gain_hbm,
    w_in_hbm, w_out_hbm, id_hbm, gate_hbm,
    out_ref, memory_ref,
    start_ref, layer_ref, enc_ref, enc_gain_ref, dec_ref, q_ref, w_ref, ffn_gain_ref, w_in, w_out, id_ref, gate_ref,
    raw, win, mem, w0, wz, qg, part, pr, ds, dbuf, d1, g, y, rb, rz, rt, d2, ret,
    load_sem, wx_s, wx_r, raw_s, raw_r, win_s, win_r, q_s, q_r, self_sem,
    xr_s, xr_r, xl_s, xl_r, x2_s, x2_r, sib_s, sib_r, zr_s, zr_r, zl_s, zl_r,
    p_s, p_r, d1_s, d1_r, g_s, g_r, gs_s, gs_r, rb_s, rb_r, rz_s, rz_r, d2_s, d2_r,
):
    width = enc_ref.shape[0]

    moves = [
        (w_hbm, w_ref), (enc_hbm, enc_ref), (q_hbm, q_ref), (enc_gain_hbm, enc_gain_ref.at[0]),
        (dec_hbm, dec_ref), (ffn_gain_hbm, ffn_gain_ref), (id_hbm, id_ref), (gate_hbm, gate_ref),
        (w_in_hbm, w_in), (w_out_hbm, w_out), (start_hbm, start_ref), (layer_hbm, layer_ref),
    ]
    loads = [pltpu.make_async_copy(a, b, load_sem.at[i]) for i, (a, b) in enumerate(moves)]
    for d in loads:
        d.start()

    s = lax.axis_index("section")
    e = lax.axis_index("expert")
    c = lax.rem(e, 2)
    z = lax.rem(e // 2, 8)
    x = lax.rem(e // 16, 4)
    yh = e // 64
    zh, zl = z // 4, lax.rem(z, 4)

    def at(yy, xx, zz, cc, ss=None):
        return (s if ss is None else ss, ((yy * 4 + xx) * 8 + zz) * 2 + cc)

    def mod(v, n):
        return lax.rem(v + n, n)

    sibling = at(yh, x, z, 1 - c)
    right, left = at(yh, mod(x + 1, 4), z, c), at(yh, mod(x - 1, 4), z, c)
    up, down = at(yh, x, mod(z + 1, 8), c), at(yh, x, mod(z - 1, 8), c)
    me8 = x * 2 + c
    me16 = yh * 8 + x * 2 + zh
    role = [(dx, dc) for dx in range(4) for dc in range(2)]

    def role_of(dx, dc):
        xx = mod(x + dx, 4)
        cc = lax.rem(c + dc, 2)
        return xx, cc

    def expert_of(i):
        yy = lax.rem(yh + i // 8, 2)
        xx = mod(x + (i // 2) % 4, 4)
        if i % 2:
            zz_h, zz_l = 1 - zh, 3 - zl
        else:
            zz_h, zz_l = zh, zl
        return yy * 8 + xx * 2 + zz_h, at(yy, xx, zz_h * 4 + zz_l, c)

    pending = []

    def copy(src, dst, ssem, rsem, dev):
        return pltpu.make_async_remote_copy(
            src_ref=src, dst_ref=dst, send_sem=ssem, recv_sem=rsem, device_id=dev,
            device_id_type=pl.DeviceIdType.MESH,
        )

    def send(src, dst, ssem, rsem, dev):
        d = copy(src, dst, ssem, rsem, dev)
        d.start()
        pending.append(d)

    def arrived(dst, rsem):
        copy(dst, dst, rsem, rsem, sibling).wait_recv()

    barrier = pltpu.get_barrier_semaphore()
    peers = [at(yh, x, z, c, lax.rem(s + k, 4)) for k in (1, 2, 3)]
    peers += [at(yh, *role_of(dx, dc)[:1], z, role_of(dx, dc)[1]) for dx, dc in role[1:]]
    peers += [up, down]
    peers += [at(1 - yh, x, z, cc) for cc in (0, 1)]
    peers += [at(yh, x, zh * 4 + lax.rem(zl + k, 4), c) for k in (1, 2, 3)]
    peers += [expert_of(i)[1] for i in range(1, 16)]
    for dev in peers:
        pl.semaphore_signal(barrier, inc=1, device_id=dev, device_id_type=pl.DeviceIdType.MESH)

    loads[10].wait()
    loads[11].wait()
    start = start_ref[0]
    layer = layer_ref[0]
    loads[0].wait()
    loads[1].wait()

    @pl.when(s == 0)
    def _():
        row = lax.broadcasted_iota(jnp.int32, (128, 128), 0)
        col = lax.broadcasted_iota(jnp.int32, (128, 128), 1)
        turn = (col == row).astype(F32).astype(BF)
        raw[...] = dot(turn, enc_ref[...], NT).astype(BF).reshape(8, CHUNK, width)

    @pl.when(s > 0)
    def _():
        row = lax.broadcasted_iota(jnp.int32, (16, 128), 0)
        col = lax.broadcasted_iota(jnp.int32, (16, 128), 1)
        pick = ((col == row + start) & (row < PATCH)).astype(F32).astype(BF)
        win[s - 1] = dot(pick, enc_ref[...], NT).astype(BF)

    pl.semaphore_wait(barrier, len(peers))

    for yy in (0, 1):
        here = (yh == yy) & (c == yh)

        @pl.when(here)
        def _(yy=yy):
            pltpu.make_async_copy(w_ref, w0.at[c], self_sem.at[0]).start()

        @pl.when(jnp.logical_not(here))
        def _(yy=yy):
            copy(w_ref, w0.at[c], wx_s.at[yy], wx_r.at[c], at(yy, x, z, yh)).start()

    @pl.when(s == 0)
    def _():
        for k in range(8):
            copy(raw.at[k], raw.at[k], raw_s.at[k], raw_r.at[k], at(yh, x, z, c, 1)).start()

    @pl.when(s > 0)
    def _():
        for k in (1, 2, 3):
            copy(
                win.at[s - 1], win.at[s - 1], win_s.at[k - 1], win_r.at[s - 1],
                at(yh, x, z, c, lax.rem(s + k, 4)),
            ).start()

    loads[2].wait()
    loads[3].wait()
    for i, (dx, dc) in enumerate(role):
        xx, cc = role_of(dx, dc)
        cols = pl.ds(pl.multiple_of((cc * 4 + xx) * 128, 128), 128)
        if i == 0:
            qg[me8] = q_ref[:, cols]
        else:
            send(q_ref.at[:, cols], qg.at[me8], q_s.at[i], q_r.at[i], at(yh, xx, z, cc))

    q_left, q_right, q_far = (mod(x + d, 4) * 2 + c for d in (3, 1, 2))

    def go(src, dst, ssem, rsem, dev):
        copy(src, dst, ssem, rsem, dev).start()

    def patched_chunk(k):
        @pl.when(s > 0)
        def _():
            arrived(raw.at[k], raw_r.at[k])

        @pl.when((s > 0) & (s < 3))
        def _():
            go(raw.at[k], raw.at[k], raw_s.at[k], raw_r.at[k], at(yh, x, z, c, s + 1))

        for i in range(3):
            @pl.when((s != i + 1) & (k == 0))
            def _(i=i):
                arrived(win.at[i], win_r.at[i])

        first = k * CHUNK - start
        row = lax.broadcasted_iota(jnp.int32, (CHUNK, 16), 0) + first
        slot = lax.broadcasted_iota(jnp.int32, (CHUNK, 16), 1)
        pick = ((row == slot) & (slot < PATCH)).astype(F32).astype(BF)
        window = jnp.where(layer == 1, win[0], jnp.where(layer == 2, win[1], win[2]))
        fresh = dot(pick, window)
        at_row = lax.broadcasted_iota(jnp.int32, fresh.shape, 0) + first
        values = jnp.where((at_row >= 0) & (at_row < PATCH), fresh, raw[k].astype(F32))
        scale = lax.rsqrt(jnp.mean(values * values, axis=-1, keepdims=True) + EPS)
        normed = (values * scale * enc_gain_ref[...]).astype(BF)
        mem[me8, k] = normed
        memory_ref[k] = normed
        block = mem.at[me8, k]
        go(block, block, xr_s.at[k], xr_r.at[k], right)
        go(block, block, xl_s.at[k], xl_r.at[k], left)
        go(block, block, sib_s.at[0, k], sib_r.at[0, k], sibling)

    def neighbour_chunk(k):
        block = mem.at[q_left, k]
        arrived(block, xr_r.at[k])

        @pl.when(k < 4)
        def _():
            go(block, block, x2_s.at[k], x2_r.at[k], right)

        go(block, block, sib_s.at[3, k], sib_r.at[3, k], sibling)
        other = mem.at[q_right, k]
        arrived(other, xl_r.at[k])

        @pl.when(k >= 4)
        def _():
            go(other, other, x2_s.at[k], x2_r.at[k], left)

        go(other, other, sib_s.at[1, k], sib_r.at[1, k], sibling)

    def far_chunk(k):
        block = mem.at[q_far, k]
        arrived(block, x2_r.at[k])
        go(block, block, sib_s.at[2, k], sib_r.at[2, k], sibling)

    def ring_up(r, m):
        block = wz.at[m, mod(z - r + 8, 8)]
        go(block, block, zr_s.at[r, m], zr_r.at[r, m], up)

    def ring_down(r, m):
        block = wz.at[m, mod(z + r, 8)]
        go(block, block, zl_s.at[r, m], zl_r.at[r, m], down)

    def from_down(r, m):
        arrived(wz.at[m, mod(z - r + 7, 8)], zr_r.at[r, m])

    def from_up(r, m):
        arrived(wz.at[m, mod(z + r + 1, 8)], zl_r.at[r, m])

    def own_weights():
        for cc in (0, 1):
            here = (c == yh) & (c == cc)

            @pl.when(here)
            def _(cc=cc):
                pltpu.make_async_copy(w_ref, w0.at[cc], self_sem.at[0]).wait()

            @pl.when(jnp.logical_not(here))
            def _(cc=cc):
                arrived(w0.at[cc], wx_r.at[cc])

        for m in range(3):
            both = jnp.concatenate([w0[0, m].astype(F32), w0[1, m].astype(F32)], axis=0)
            wz[m, z] = both.astype(BF)
            ring_up(0, m)
            ring_down(0, m)

    first_a = 2 * s
    first_w, first_z = 3, 5

    def tick(t, carry):
        k = t - first_a

        @pl.when((k >= 0) & (k < 8))
        def _():
            patched_chunk(k)

        @pl.when(t == first_w)
        def _():
            own_weights()

        kb = k - 3

        @pl.when((kb >= 0) & (kb < 8))
        def _():
            neighbour_chunk(kb)

        j = t - first_z
        r, m = j // 3, lax.rem(j, 3)

        @pl.when((j >= 0) & (j < 8))
        def _():
            from_down(r, m)
            ring_up(r + 1, m)

        @pl.when((j >= 0) & ((j < 6) | (j == 8)))
        def _():
            from_up(r, m)
            ring_down(r + 1, m)

        return carry

    lax.fori_loop(0, 17, tick, 0)
    from_down(2, 2), from_down(3, 0), from_down(3, 1)
    from_up(2, 0), from_up(2, 1), from_up(3, 2)
    for i, (dx, dc) in enumerate(role[1:], 1):
        arrived(qg.at[mod(x - dx, 4) * 2 + lax.rem(c + dc, 2)], q_r.at[i])

    first_head = lax.broadcasted_iota(jnp.int32, (16, 128), 1) < HEAD_DIM

    def attend(dx):
        xx = mod(x + dx, 4)
        for k in range(8):
            arrived(mem.at[xx * 2 + (1 - c), k], sib_r.at[dx, k])
        rows = mem[pl.ds(xx * 2, 2)].reshape(256, width)
        kv = dot(rows, wz[0:2].reshape(256, width), NT).astype(BF)
        for cc in (0, 1):
            q = xx * 2 + cc
            keys, values = kv[cc * 128:cc * 128 + 128, :128], kv[cc * 128:cc * 128 + 128, 128:]
            ask = qg[q].astype(F32)
            ask = jnp.concatenate(
                [jnp.where(first_head, ask, 0.0), jnp.where(first_head, 0.0, ask)], axis=0
            )
            exponent = jnp.exp(dot(ask.astype(BF), keys, NT))
            shares = exponent / jnp.sum(exponent, axis=-1, keepdims=True)
            mixed = dot(shares.astype(BF), values)
            context = jnp.where(first_head, mixed[:16], mixed[16:]).astype(BF)
            part[q] = dot(context, wz[2].reshape(128, width)).astype(BF)
        for dc in (0, 1):
            i = dx * 2 + dc
            cc = lax.rem(c + dc, 2)
            if i:
                send(part.at[xx * 2 + cc], pr.at[me8], p_s.at[i], p_r.at[i], at(yh, xx, z, cc))

    attend(0)
    for k in range(4):
        far_chunk(k)
    attend(3)
    for k in range(4, 8):
        far_chunk(k)
    attend(1)
    attend(2)

    for d in loads[4:10]:
        d.wait()
    total = dec_ref[...].astype(F32) + part[me8].astype(F32)
    for i, (dx, dc) in enumerate(role[1:], 1):
        q = mod(x - dx, 4) * 2 + lax.rem(c + dc, 2)
        arrived(pr.at[q], p_r.at[i])
        total = total + pr[q].astype(F32)
    residual = total.astype(BF)
    total = residual.astype(F32)
    scale = lax.rsqrt(jnp.mean(total * total, axis=-1, keepdims=True) + EPS)
    normed = (total * scale * ffn_gain_ref[...]).astype(BF)

    row = lax.broadcasted_iota(jnp.int32, (16, 16), 0)
    col = lax.broadcasted_iota(jnp.int32, (16, 16), 1)
    id_row = jnp.broadcast_to(id_ref[...], (16, 16)).astype(F32)
    id_col = jnp.sum(jnp.where(row == col, id_row, 0.0), axis=1, keepdims=True)
    gate = jnp.broadcast_to(gate_ref[...], (16, 16))
    gate = jnp.sum(jnp.where(row == col, gate, 0.0), axis=1, keepdims=True)
    id_row = id_row[0:1]
    same = (jnp.broadcast_to(id_row, (16, 16)) == jnp.broadcast_to(id_col, (16, 16))).astype(F32)
    slot_row = jnp.sum(jnp.where(row < col, same, 0.0), axis=0, keepdims=True)
    slot_col = jnp.sum(jnp.where(col < row, same, 0.0), axis=1, keepdims=True)
    number = lax.broadcasted_iota(jnp.int32, (32, 16), 0)
    chosen = (lax.rem(number, 16).astype(F32) == id_row) & ((number // 16).astype(F32) == slot_row)
    picked = dot(chosen.astype(F32).astype(BF), normed)
    ds[:, 0, :] = picked[:16]
    ds[:, 1, :] = picked[16:]
    dbuf[...] = ds[...].astype(BF)

    for i in range(1, 16):
        block, dev = expert_of(i)
        send(dbuf.at[block], d1.at[me16], d1_s.at[i], d1_r.at[i], dev)
    d1[me16] = dbuf[me16]

    def back(i):
        yy = lax.rem(yh + i // 8, 2)
        xx = mod(x - (i // 2) % 4, 4)
        return yy * 8 + xx * 2 + (1 - zh if i % 2 else zh)

    for i in range(1, 16):
        arrived(d1.at[back(i)], d1_r.at[i])
    ds[...] = d1[...].astype(F32)
    g[zl, c] = jnp.concatenate([ds[:, 0, :], ds[:, 1, :]], axis=0).astype(BF)

    block = g.at[zl, c]
    for k in (1, 2, 3):
        send(block, block, g_s.at[k], g_r.at[k], at(yh, x, zh * 4 + lax.rem(zl + k, 4), c))
    send(block, block, gs_s.at[0], gs_r.at[0], sibling)
    for k in (1, 2, 3):
        block = g.at[mod(zl - k, 4), c]
        arrived(block, g_r.at[k])
        send(block, block, gs_s.at[k], gs_r.at[k], sibling)
    for k in range(4):
        arrived(g.at[mod(zl - k, 4), 1 - c], gs_r.at[k])

    hidden = jnp.maximum(dot(g[...].reshape(256, width), w_in[...]), 0.0).astype(BF)
    y[...] = dot(hidden, w_out[...], NT).astype(BF).reshape(y.shape)

    order = (1, 2, 3, 0)
    for k in order:
        to = lax.rem(zl + k, 4)
        send(y.at[to, 1 - c], rb.at[to], rb_s.at[k], rb_r.at[k], sibling)
    for k in order:
        to = lax.rem(zl + k, 4)
        arrived(rb.at[to], rb_r.at[k])
        pair = y[to, c].astype(F32) + rb[to].astype(F32)
        if k:
            rt[to] = pair.astype(BF)
            send(rt.at[to], rz.at[zl], rz_s.at[k], rz_r.at[k], at(yh, x, zh * 4 + to, c))
        else:
            total = pair
    for k in (1, 2, 3):
        src = mod(zl - k, 4)
        arrived(rz.at[src], rz_r.at[k])
        total = total + rz[src].astype(F32)
    ds[:, 0, :] = total[:16]
    ds[:, 1, :] = total[16:]
    d2[...] = ds[...].astype(BF)
    for i in range(1, 16):
        block, dev = expert_of(i)
        send(d2.at[block], ret.at[me16], d2_s.at[i], d2_r.at[i], dev)
    ret[me16] = d2[me16]
    for i in range(1, 16):
        arrived(ret.at[back(i)], d2_r.at[i])
    ds[...] = ret[...].astype(F32)
    slots = jnp.concatenate([ds[:, 0, :], ds[:, 1, :]], axis=0).astype(BF)
    number = lax.broadcasted_iota(jnp.int32, (16, 32), 1)
    chosen = (lax.rem(number, 16).astype(F32) == id_col) & ((number // 16).astype(F32) == slot_col)
    combined = dot(chosen.astype(F32).astype(BF), slots)
    out_ref[...] = (residual.astype(F32) + gate * combined).astype(BF)

    for d in pending:
        d.wait_send()
    for yy in (0, 1):
        @pl.when(jnp.logical_not((yh == yy) & (c == yh)))
        def _(yy=yy):
            copy(w_ref, w0.at[c], wx_s.at[yy], wx_r.at[c], at(yy, x, z, yh)).wait_send()

    @pl.when(s < 3)
    def _():
        for k in range(8):
            copy(raw.at[k], raw.at[k], raw_s.at[k], raw_r.at[k], sibling).wait_send()

    @pl.when(s > 0)
    def _():
        for k in (1, 2, 3):
            copy(
                win.at[s - 1], win.at[s - 1], win_s.at[k - 1], win_r.at[s - 1], sibling
            ).wait_send()

    def sent(ref, sem):
        copy(ref, ref, sem, sem, sibling).wait_send()

    for k in range(8):
        for sem in (xr_s, xl_s, x2_s):
            sent(mem.at[me8, k], sem.at[k])
        for d in range(4):
            sent(mem.at[me8, k], sib_s.at[d, k])
    for r in range(4):
        for m in range(3):
            if r < 3 or m < 2:
                sent(wz.at[m, z], zr_s.at[r, m])
            if r < 3 or m == 2:
                sent(wz.at[m, z], zl_s.at[r, m])


def per_device(
    enc_states, patch_start, patch_layer, enc_gain, dec_states, queries, attn_weight, ffn_gain,
    expert_in, expert_out, expert_id, gate,
):
    rows, width = enc_states.shape[1:]
    hid = expert_in.shape[-1]
    dma = lambda *shape: pltpu.SemaphoreType.DMA(shape)
    vm = lambda *shape: pltpu.VMEM(shape, BF)
    vmem = pl.BlockSpec(memory_space=pltpu.VMEM)
    hbm = pl.BlockSpec(memory_space=pltpu.HBM)
    scratch = [
        pltpu.SMEM((1,), jnp.int32), pltpu.SMEM((1,), jnp.int32),
        vm(width, rows), pltpu.VMEM((1, width), F32), vm(16, width), vm(16, 1024), vm(3, 8, width),
        pltpu.VMEM((1, width), F32), vm(width, hid), vm(width, hid),
        pltpu.VMEM((1, 16), jnp.int32), pltpu.VMEM((1, 16), F32),
        vm(8, 16, width), vm(3, 16, width), vm(8, 8, 16, width), vm(2, 3, 8, width),
        vm(3, 8, 16, width), vm(8, 16, 128), vm(8, 16, width), vm(8, 16, width),
        pltpu.VMEM((16, 2, width), F32), vm(16, 2, width), vm(16, 2, width),
        vm(4, 2, 32, width), vm(4, 2, 32, width), vm(4, 32, width), vm(4, 32, width),
        vm(4, 32, width), vm(16, 2, width), vm(16, 2, width),
        dma(12), dma(2), dma(2), dma(8), dma(8), dma(3), dma(3), dma(8), dma(8), dma(1),
        dma(8), dma(8), dma(8), dma(8), dma(8), dma(8), dma(4, 8), dma(4, 8),
        dma(4, 3), dma(4, 3), dma(4, 3), dma(4, 3),
        dma(8), dma(8), dma(16), dma(16), dma(4), dma(4), dma(4), dma(4), dma(4), dma(4),
        dma(4), dma(4), dma(16), dma(16),
    ]
    out, memory = pl.pallas_call(
        kernel,
        out_shape=(
            jax.ShapeDtypeStruct(dec_states.shape[1:], BF),
            jax.ShapeDtypeStruct((8, 16, width), BF),
        ),
        in_specs=[hbm] * 12,
        out_specs=(vmem, vmem),
        scratch_shapes=scratch,
        compiler_params=pltpu.CompilerParams(
            collective_id=0, has_side_effects=True, vmem_limit_bytes=60 * 1024 * 1024
        ),
    )(
        patch_start, patch_layer, enc_states[0].T, enc_gain, dec_states[0], queries[0],
        jnp.transpose(attn_weight[0], (0, 2, 1)), ffn_gain, expert_in[0, 0], expert_out[0, 0].T,
        expert_id[0].reshape(1, 16), gate,
    )
    return out[None], memory.reshape(rows, width)


def solution(mesh):
    in_specs = (
        P("section", "expert", None),
        P("expert"),
        P("expert"),
        P(),
        P("section", "expert", None),
        P("section", "expert", None),
        P("section", None, None, "expert"),
        P("section", None),
        P("section", "expert", None, None),
        P("section", "expert", None, None),
        P("section", "expert", None),
        P("section", "expert"),
    )
    out_specs = (P("section", "expert", None), P("expert", None))
    return jax.shard_map(
        per_device, mesh=mesh, in_specs=in_specs, out_specs=out_specs, check_vma=False
    )
```

```python
import jax
import jax.numpy as jnp
from jax import lax
from jax.experimental import pallas as pl
from jax.experimental.pallas import tpu as pltpu
from jax.sharding import PartitionSpec as P

HEAD_DIM = 64
PATCH = 8
CHUNK = 16
EPS = 1e-06
BF, F32 = jnp.bfloat16, jnp.float32
NT = (((1,), (1,)), ((), ()))
NN = (((1,), (0,)), ((), ()))


def dot(a, b, dims=NN):
    return lax.dot_general(a, b, dims, preferred_element_type=F32)


def kernel(
    start_hbm, layer_hbm, enc_hbm, enc_gain_hbm, dec_hbm, q_hbm, w_hbm, ffn_gain_hbm,
    w_in_hbm, w_out_hbm, id_hbm, gate_hbm,
    out_ref, memory_ref,
    start_ref, layer_ref, enc_ref, enc_gain_ref, dec_ref, q_ref, w_ref, ffn_gain_ref, w_in, w_out, id_ref, gate_ref,
    raw, win, mem, w0, wz, qg, part, pr, ds, dbuf, d1, g, y, rb, rz, rt, d2, ret,
    load_sem, wx_s, wx_r, raw_s, raw_r, win_s, win_r, q_s, q_r, self_sem,
    xr_s, xr_r, xl_s, xl_r, x2_s, x2_r, sib_s, sib_r, zr_s, zr_r, zl_s, zl_r,
    p_s, p_r, d1_s, d1_r, g_s, g_r, gs_s, gs_r, rb_s, rb_r, rz_s, rz_r, d2_s, d2_r,
):
    width = enc_ref.shape[0]

    moves = [
        (w_hbm, w_ref), (enc_hbm, enc_ref), (q_hbm, q_ref), (enc_gain_hbm, enc_gain_ref.at[0]),
        (dec_hbm, dec_ref), (ffn_gain_hbm, ffn_gain_ref), (id_hbm, id_ref), (gate_hbm, gate_ref),
        (w_in_hbm, w_in), (w_out_hbm, w_out), (start_hbm, start_ref), (layer_hbm, layer_ref),
    ]
    loads = [pltpu.make_async_copy(a, b, load_sem.at[i]) for i, (a, b) in enumerate(moves)]
    for d in loads:
        d.start()

    s = lax.axis_index("section")
    e = lax.axis_index("expert")
    c = lax.rem(e, 2)
    z = lax.rem(e // 2, 8)
    x = lax.rem(e // 16, 4)
    yh = e // 64
    zh, zl = z // 4, lax.rem(z, 4)

    def at(yy, xx, zz, cc, ss=None):
        return (s if ss is None else ss, ((yy * 4 + xx) * 8 + zz) * 2 + cc)

    def mod(v, n):
        return lax.rem(v + n, n)

    sibling = at(yh, x, z, 1 - c)
    right, left = at(yh, mod(x + 1, 4), z, c), at(yh, mod(x - 1, 4), z, c)
    up, down = at(yh, x, mod(z + 1, 8), c), at(yh, x, mod(z - 1, 8), c)
    me8 = x * 2 + c
    me16 = yh * 8 + x * 2 + zh
    side, odd = zl // 2, lax.rem(zl, 2)
    me32 = me16 * 2 + side
    role = [(dx, dc) for dx in range(4) for dc in range(2)]

    def role_of(dx, dc):
        xx = mod(x + dx, 4)
        cc = lax.rem(c + dc, 2)
        return xx, cc

    def partner(i, h):
        yy = lax.rem(yh + i // 8, 2)
        xx = mod(x + (i // 2) % 4, 4)
        zz_h, zz_l = (1 - zh, 1 - odd) if i % 2 else (zh, odd)
        return yy * 8 + xx * 2 + zz_h, at(yy, xx, zz_h * 4 + zz_l + 2 * h, c)

    def source(i):
        yy = lax.rem(yh + i // 8, 2)
        xx = mod(x - (i // 2) % 4, 4)
        return yy * 8 + xx * 2 + (1 - zh if i % 2 else zh)

    pending = []

    def copy(src, dst, ssem, rsem, dev):
        return pltpu.make_async_remote_copy(
            src_ref=src, dst_ref=dst, send_sem=ssem, recv_sem=rsem, device_id=dev,
            device_id_type=pl.DeviceIdType.MESH,
        )

    def send(src, dst, ssem, rsem, dev):
        d = copy(src, dst, ssem, rsem, dev)
        d.start()
        pending.append(d)

    def arrived(dst, rsem):
        copy(dst, dst, rsem, rsem, sibling).wait_recv()

    barrier = pltpu.get_barrier_semaphore()
    peers = [at(yh, x, z, c, lax.rem(s + k, 4)) for k in (1, 2, 3)]
    peers += [at(yh, *role_of(dx, dc)[:1], z, role_of(dx, dc)[1]) for dx, dc in role[1:]]
    peers += [up, down]
    peers += [at(1 - yh, x, z, cc) for cc in (0, 1)]
    for dev in peers:
        pl.semaphore_signal(barrier, inc=1, device_id=dev, device_id_type=pl.DeviceIdType.MESH)

    loads[10].wait()
    loads[11].wait()
    start = start_ref[0]
    layer = layer_ref[0]
    loads[0].wait()
    loads[1].wait()

    @pl.when(s == 0)
    def _():
        row = lax.broadcasted_iota(jnp.int32, (128, 128), 0)
        col = lax.broadcasted_iota(jnp.int32, (128, 128), 1)
        turn = (col == row).astype(F32).astype(BF)
        raw[...] = dot(turn, enc_ref[...], NT).astype(BF).reshape(8, CHUNK, width)

    @pl.when(s > 0)
    def _():
        row = lax.broadcasted_iota(jnp.int32, (16, 128), 0)
        col = lax.broadcasted_iota(jnp.int32, (16, 128), 1)
        pick = ((col == row + start) & (row < PATCH)).astype(F32).astype(BF)
        win[s - 1] = dot(pick, enc_ref[...], NT).astype(BF)

    pl.semaphore_wait(barrier, len(peers))

    for yy in (0, 1):
        here = (yh == yy) & (c == yh)

        @pl.when(here)
        def _(yy=yy):
            pltpu.make_async_copy(w_ref, w0.at[c], self_sem.at[0]).start()

        @pl.when(jnp.logical_not(here))
        def _(yy=yy):
            copy(w_ref, w0.at[c], wx_s.at[yy], wx_r.at[c], at(yy, x, z, yh)).start()

    @pl.when(s == 0)
    def _():
        for k in range(8):
            copy(raw.at[k], raw.at[k], raw_s.at[k], raw_r.at[k], at(yh, x, z, c, 1)).start()

    @pl.when(s > 0)
    def _():
        for k in (1, 2, 3):
            copy(
                win.at[s - 1], win.at[s - 1], win_s.at[k - 1], win_r.at[s - 1],
                at(yh, x, z, c, lax.rem(s + k, 4)),
            ).start()

    loads[2].wait()
    loads[3].wait()
    for i, (dx, dc) in enumerate(role):
        xx, cc = role_of(dx, dc)
        cols = pl.ds(pl.multiple_of((cc * 4 + xx) * 128, 128), 128)
        if i == 0:
            qg[me8] = q_ref[:, cols]
        else:
            send(q_ref.at[:, cols], qg.at[me8], q_s.at[i], q_r.at[i], at(yh, xx, z, cc))

    q_left, q_right, q_far = (mod(x + d, 4) * 2 + c for d in (3, 1, 2))

    def go(src, dst, ssem, rsem, dev):
        copy(src, dst, ssem, rsem, dev).start()

    def patched_chunk(k):
        @pl.when(s > 0)
        def _():
            arrived(raw.at[k], raw_r.at[k])

        @pl.when((s > 0) & (s < 3))
        def _():
            go(raw.at[k], raw.at[k], raw_s.at[k], raw_r.at[k], at(yh, x, z, c, s + 1))

        for i in range(3):
            @pl.when((s != i + 1) & (k == 0))
            def _(i=i):
                arrived(win.at[i], win_r.at[i])

        first = k * CHUNK - start
        row = lax.broadcasted_iota(jnp.int32, (CHUNK, 16), 0) + first
        slot = lax.broadcasted_iota(jnp.int32, (CHUNK, 16), 1)
        pick = ((row == slot) & (slot < PATCH)).astype(F32).astype(BF)
        window = jnp.where(layer == 1, win[0], jnp.where(layer == 2, win[1], win[2]))
        fresh = dot(pick, window)
        at_row = lax.broadcasted_iota(jnp.int32, fresh.shape, 0) + first
        values = jnp.where((at_row >= 0) & (at_row < PATCH), fresh, raw[k].astype(F32))
        scale = lax.rsqrt(jnp.mean(values * values, axis=-1, keepdims=True) + EPS)
        normed = (values * scale * enc_gain_ref[...]).astype(BF)
        mem[me8, k] = normed
        block = mem.at[me8, k]
        go(block, block, xr_s.at[k], xr_r.at[k], right)
        go(block, block, xl_s.at[k], xl_r.at[k], left)
        go(block, block, sib_s.at[0, k], sib_r.at[0, k], sibling)

    def neighbour_chunk(k):
        block = mem.at[q_left, k]
        arrived(block, xr_r.at[k])

        @pl.when(k < 4)
        def _():
            go(block, block, x2_s.at[k], x2_r.at[k], right)

        go(block, block, sib_s.at[3, k], sib_r.at[3, k], sibling)
        other = mem.at[q_right, k]
        arrived(other, xl_r.at[k])

        @pl.when(k >= 4)
        def _():
            go(other, other, x2_s.at[k], x2_r.at[k], left)

        go(other, other, sib_s.at[1, k], sib_r.at[1, k], sibling)

    def far_chunk(k):
        block = mem.at[q_far, k]
        arrived(block, x2_r.at[k])
        go(block, block, sib_s.at[2, k], sib_r.at[2, k], sibling)

    def ring_up(r, m):
        block = wz.at[m, mod(z - r + 8, 8)]
        go(block, block, zr_s.at[r, m], zr_r.at[r, m], up)

    def ring_down(r, m):
        block = wz.at[m, mod(z + r, 8)]
        go(block, block, zl_s.at[r, m], zl_r.at[r, m], down)

    def from_down(r, m):
        arrived(wz.at[m, mod(z - r + 7, 8)], zr_r.at[r, m])

    def from_up(r, m):
        arrived(wz.at[m, mod(z + r + 1, 8)], zl_r.at[r, m])

    def own_weights():
        for cc in (0, 1):
            here = (c == yh) & (c == cc)

            @pl.when(here)
            def _(cc=cc):
                pltpu.make_async_copy(w_ref, w0.at[cc], self_sem.at[0]).wait()

            @pl.when(jnp.logical_not(here))
            def _(cc=cc):
                arrived(w0.at[cc], wx_r.at[cc])

        for m in range(3):
            both = jnp.concatenate([w0[0, m].astype(F32), w0[1, m].astype(F32)], axis=0)
            wz[m, z] = both.astype(BF)
            ring_up(0, m)
            ring_down(0, m)

    first_a = 2 * s
    first_w = jnp.where(c == yh, 0, jnp.where(s == 0, 8, 5))
    first_z = first_w + 2

    def tick(t, carry):
        k = t - first_a

        @pl.when((k >= 0) & (k < 8))
        def _():
            patched_chunk(k)

        @pl.when(t == first_w)
        def _():
            own_weights()

        kb = k - 3

        @pl.when((kb >= 0) & (kb < 8))
        def _():
            neighbour_chunk(kb)

        j = t - first_z
        r, m = j // 3, lax.rem(j, 3)

        @pl.when((j >= 0) & (j < 8))
        def _():
            from_down(r, m)
            ring_up(r + 1, m)

        @pl.when((j >= 0) & ((j < 6) | (j == 8)))
        def _():
            from_up(r, m)
            ring_down(r + 1, m)

        return carry

    lax.fori_loop(0, 20, tick, 0)
    from_down(2, 2), from_down(3, 0), from_down(3, 1)
    from_up(2, 0), from_up(2, 1), from_up(3, 2)
    for i, (dx, dc) in enumerate(role[1:], 1):
        arrived(qg.at[mod(x - dx, 4) * 2 + lax.rem(c + dc, 2)], q_r.at[i])

    first_head = lax.broadcasted_iota(jnp.int32, (16, 128), 1) < HEAD_DIM

    def attend(dx):
        xx = mod(x + dx, 4)
        for k in range(8):
            arrived(mem.at[xx * 2 + (1 - c), k], sib_r.at[dx, k])
        rows = mem[pl.ds(xx * 2, 2)].reshape(256, width)
        kv = dot(rows, wz[0:2].reshape(256, width), NT).astype(BF)
        for cc in (0, 1):
            q = xx * 2 + cc
            keys, values = kv[cc * 128:cc * 128 + 128, :128], kv[cc * 128:cc * 128 + 128, 128:]
            ask = qg[q].astype(F32)
            ask = jnp.concatenate(
                [jnp.where(first_head, ask, 0.0), jnp.where(first_head, 0.0, ask)], axis=0
            )
            exponent = jnp.exp(dot(ask.astype(BF), keys, NT))
            shares = exponent / jnp.sum(exponent, axis=-1, keepdims=True)
            mixed = dot(shares.astype(BF), values)
            context = jnp.where(first_head, mixed[:16], mixed[16:]).astype(BF)
            part[q] = dot(context, wz[2].reshape(128, width)).astype(BF)
        for dc in (0, 1):
            i = dx * 2 + dc
            cc = lax.rem(c + dc, 2)
            if i:
                send(part.at[xx * 2 + cc], pr.at[me8], p_s.at[i], p_r.at[i], at(yh, xx, z, cc))

    attend(0)
    for k in range(4):
        far_chunk(k)
    attend(3)
    for k in range(4, 8):
        far_chunk(k)
    attend(1)
    attend(2)

    row = lax.broadcasted_iota(jnp.int32, (128, 128), 0)
    col = lax.broadcasted_iota(jnp.int32, (128, 128), 1)
    turn = (col == row).astype(F32).astype(BF)
    memory_ref[...] = dot(mem[me8].reshape(128, width), turn, (((0,), (0,)), ((), ()))).astype(BF)
    for d in loads[4:10]:
        d.wait()
    total = dec_ref[...].astype(F32) + part[me8].astype(F32)
    for i, (dx, dc) in enumerate(role[1:], 1):
        q = mod(x - dx, 4) * 2 + lax.rem(c + dc, 2)
        arrived(pr.at[q], p_r.at[i])
        total = total + pr[q].astype(F32)
    residual = total.astype(BF)
    total = residual.astype(F32)
    scale = lax.rsqrt(jnp.mean(total * total, axis=-1, keepdims=True) + EPS)
    normed = (total * scale * ffn_gain_ref[...]).astype(BF)

    row = lax.broadcasted_iota(jnp.int32, (16, 16), 0)
    col = lax.broadcasted_iota(jnp.int32, (16, 16), 1)
    id_row = jnp.broadcast_to(id_ref[...], (16, 16)).astype(F32)
    id_col = jnp.sum(jnp.where(row == col, id_row, 0.0), axis=1, keepdims=True)
    gate = jnp.broadcast_to(gate_ref[...], (16, 16))
    gate = jnp.sum(jnp.where(row == col, gate, 0.0), axis=1, keepdims=True)
    id_row = id_row[0:1]
    same = (jnp.broadcast_to(id_row, (16, 16)) == jnp.broadcast_to(id_col, (16, 16))).astype(F32)
    slot_row = jnp.sum(jnp.where(row < col, same, 0.0), axis=0, keepdims=True)
    slot_col = jnp.sum(jnp.where(col < row, same, 0.0), axis=1, keepdims=True)
    number = lax.broadcasted_iota(jnp.int32, (32, 16), 0)
    chosen = (lax.rem(number, 16).astype(F32) == id_row) & ((number // 16).astype(F32) == slot_row)
    picked = dot(chosen.astype(F32).astype(BF), normed)
    ds[0:16, 0, :] = picked[:16]
    ds[0:16, 1, :] = picked[16:]
    dbuf[...] = ds[0:16].astype(BF)

    def exchange(block_of, dst, ssem, rsem):
        for i in range(16):
            if i == 0:
                far = lax.rem(zl + 2, 4)
                send(
                    block_of(me16, 1 - side), dst.at[me32], ssem.at[0], rsem.at[side],
                    at(yh, x, zh * 4 + far, c),
                )
            else:
                for h in (0, 1):
                    e16, dev = partner(i, h)
                    send(block_of(e16, h), dst.at[me32], ssem.at[i * 2 + h], rsem.at[i * 2 + side], dev)

    def exchanged(dst, rsem):
        arrived(dst.at[me16 * 2 + (1 - side)], rsem.at[1 - side])
        for i in range(1, 16):
            for h in (0, 1):
                arrived(dst.at[source(i) * 2 + h], rsem.at[i * 2 + h])

    exchange(lambda e16, h: dbuf.at[e16], d1, d1_s, d1_r)
    d1[me32] = dbuf[me16]
    exchanged(d1, d1_r)
    ds[...] = d1[...].astype(F32)
    g[odd, c] = jnp.concatenate([ds[:, 0, :], ds[:, 1, :]], axis=0).astype(BF)

    across = at(yh, x, zh * 4 + zl + 1 - 2 * odd, c)
    block = g.at[odd, c]
    send(block, block, g_s.at[0], g_r.at[0], across)
    send(block, block, gs_s.at[0], gs_r.at[0], sibling)
    block = g.at[1 - odd, c]
    arrived(block, g_r.at[0])
    send(block, block, gs_s.at[1], gs_r.at[1], sibling)
    arrived(g.at[odd, 1 - c], gs_r.at[0])
    arrived(g.at[1 - odd, 1 - c], gs_r.at[1])

    hidden = jnp.maximum(dot(g[...].reshape(256, width), w_in[...]), 0.0).astype(BF)
    y[...] = dot(hidden, w_out[...], NT).astype(BF).reshape(y.shape)

    for k in (0, 1):
        to = lax.rem(odd + 1 + k, 2)
        send(y.at[to, 1 - c], rb.at[to], rb_s.at[k], rb_r.at[k], sibling)
    arrived(rb.at[1 - odd], rb_r.at[0])
    rt[...] = (y[1 - odd, c].astype(F32) + rb[1 - odd].astype(F32)).astype(BF)
    send(rt, rz, rz_s.at[0], rz_r.at[0], across)
    arrived(rb.at[odd], rb_r.at[1])
    arrived(rz, rz_r.at[0])
    total = y[odd, c].astype(F32) + rb[odd].astype(F32) + rz[...].astype(F32)
    ds[:, 0, :] = total[:32]
    ds[:, 1, :] = total[32:]
    d2[...] = ds[...].astype(BF)
    exchange(lambda e16, h: d2.at[e16 * 2 + h], ret, d2_s, d2_r)
    ret[me32] = d2[me32]
    exchanged(ret, d2_r)
    ds[...] = ret[...].astype(F32)
    slots = jnp.concatenate([ds[:, 0, :], ds[:, 1, :]], axis=0).astype(BF)
    number = lax.broadcasted_iota(jnp.int32, (16, 64), 1)
    chosen = ((lax.rem(number, 32) // 2).astype(F32) == id_col) & ((number // 32).astype(F32) == slot_col)
    combined = dot(chosen.astype(F32).astype(BF), slots)
    out_ref[...] = (residual.astype(F32) + gate * combined).astype(BF)

    for d in pending:
        d.wait_send()
    for yy in (0, 1):
        @pl.when(jnp.logical_not((yh == yy) & (c == yh)))
        def _(yy=yy):
            copy(w_ref, w0.at[c], wx_s.at[yy], wx_r.at[c], at(yy, x, z, yh)).wait_send()

    @pl.when(s < 3)
    def _():
        for k in range(8):
            copy(raw.at[k], raw.at[k], raw_s.at[k], raw_r.at[k], sibling).wait_send()

    @pl.when(s > 0)
    def _():
        for k in (1, 2, 3):
            copy(
                win.at[s - 1], win.at[s - 1], win_s.at[k - 1], win_r.at[s - 1], sibling
            ).wait_send()

    def sent(ref, sem):
        copy(ref, ref, sem, sem, sibling).wait_send()

    for k in range(8):
        for sem in (xr_s, xl_s, x2_s):
            sent(mem.at[me8, k], sem.at[k])
        for d in range(4):
            sent(mem.at[me8, k], sib_s.at[d, k])
    for r in range(4):
        for m in range(3):
            if r < 3 or m < 2:
                sent(wz.at[m, z], zr_s.at[r, m])
            if r < 3 or m == 2:
                sent(wz.at[m, z], zl_s.at[r, m])


def per_device(
    enc_states, patch_start, patch_layer, enc_gain, dec_states, queries, attn_weight, ffn_gain,
    expert_in, expert_out, expert_id, gate,
):
    rows, width = enc_states.shape[1:]
    hid = expert_in.shape[-1]
    dma = lambda *shape: pltpu.SemaphoreType.DMA(shape)
    vm = lambda *shape: pltpu.VMEM(shape, BF)
    vmem = pl.BlockSpec(memory_space=pltpu.VMEM)
    hbm = pl.BlockSpec(memory_space=pltpu.HBM)
    scratch = [
        pltpu.SMEM((1,), jnp.int32), pltpu.SMEM((1,), jnp.int32),
        vm(width, rows), pltpu.VMEM((1, width), F32), vm(16, width), vm(16, 1024), vm(3, 8, width),
        pltpu.VMEM((1, width), F32), vm(width, hid), vm(width, hid),
        pltpu.VMEM((1, 16), jnp.int32), pltpu.VMEM((1, 16), F32),
        vm(8, 16, width), vm(3, 16, width), vm(8, 8, 16, width), vm(2, 3, 8, width),
        vm(3, 8, 16, width), vm(8, 16, 128), vm(8, 16, width), vm(8, 16, width),
        pltpu.VMEM((32, 2, width), F32), vm(16, 2, width), vm(32, 2, width),
        vm(2, 2, 64, width), vm(2, 2, 64, width), vm(2, 64, width), vm(64, width), vm(64, width),
        vm(32, 2, width), vm(32, 2, width),
        dma(12), dma(2), dma(2), dma(8), dma(8), dma(3), dma(3), dma(8), dma(8), dma(1),
        dma(8), dma(8), dma(8), dma(8), dma(8), dma(8), dma(4, 8), dma(4, 8),
        dma(4, 3), dma(4, 3), dma(4, 3), dma(4, 3),
        dma(8), dma(8), dma(32), dma(32), dma(1), dma(1), dma(2), dma(2), dma(2), dma(2),
        dma(1), dma(1), dma(32), dma(32),
    ]
    out, memory = pl.pallas_call(
        kernel,
        out_shape=(
            jax.ShapeDtypeStruct(dec_states.shape[1:], BF),
            jax.ShapeDtypeStruct((width, rows), BF),
        ),
        in_specs=[hbm] * 12,
        out_specs=(vmem, vmem),
        scratch_shapes=scratch,
        compiler_params=pltpu.CompilerParams(
            collective_id=0, has_side_effects=True, vmem_limit_bytes=60 * 1024 * 1024
        ),
    )(
        patch_start, patch_layer, enc_states[0].T, enc_gain, dec_states[0], queries[0],
        jnp.transpose(attn_weight[0], (0, 2, 1)), ffn_gain, expert_in[0, 0], expert_out[0, 0].T,
        expert_id[0].reshape(1, 16), gate,
    )
    return out[None], memory.T


def solution(mesh):
    in_specs = (
        P("section", "expert", None),
        P("expert"),
        P("expert"),
        P(),
        P("section", "expert", None),
        P("section", "expert", None),
        P("section", None, None, "expert"),
        P("section", None),
        P("section", "expert", None, None),
        P("section", "expert", None, None),
        P("section", "expert", None),
        P("section", "expert"),
    )
    out_specs = (P("section", "expert", None), P("expert", None))
    return jax.shard_map(
        per_device, mesh=mesh, in_specs=in_specs, out_specs=out_specs, check_vma=False
    )
```

```python
import jax
import jax.numpy as jnp
from jax import lax
from jax.experimental import pallas as pl
from jax.experimental.pallas import tpu as pltpu
from jax.sharding import PartitionSpec as P

HEAD_DIM = 64
PATCH = 8
CHUNK = 16
EPS = 1e-06
BF, F32 = jnp.bfloat16, jnp.float32
NT = (((1,), (1,)), ((), ()))
NN = (((1,), (0,)), ((), ()))


def dot(a, b, dims=NN):
    return lax.dot_general(a, b, dims, preferred_element_type=F32)


def kernel(
    start_hbm, layer_hbm, enc_hbm, enc_gain_hbm, dec_hbm, q_hbm, w_hbm, ffn_gain_hbm,
    w_in_hbm, w_out_hbm, id_hbm, gate_hbm,
    out_ref, memory_ref,
    start_ref, layer_ref, enc_ref, enc_gain_ref, dec_ref, q_ref, w_ref, ffn_gain_ref, w_in, w_out, id_ref, gate_ref,
    raw, win, mem, w0, wz, qg, part, pr, ds, dbuf, d1, g, y, rb, rz, rt, d2, ret,
    load_sem, wx_s, wx_r, raw_s, raw_r, win_s, win_r, q_s, q_r, self_sem,
    xr_s, xr_r, xl_s, xl_r, x2_s, x2_r, sib_s, sib_r, zr_s, zr_r, zl_s, zl_r,
    p_s, p_r, d1_s, d1_r, g_s, g_r, gs_s, gs_r, rb_s, rb_r, rz_s, rz_r, d2_s, d2_r,
):
    width = enc_ref.shape[0]

    moves = [
        (w_hbm, w_ref), (enc_hbm, enc_ref), (q_hbm, q_ref), (enc_gain_hbm, enc_gain_ref.at[0]),
        (dec_hbm, dec_ref), (ffn_gain_hbm, ffn_gain_ref), (id_hbm, id_ref), (gate_hbm, gate_ref),
        (w_in_hbm, w_in), (w_out_hbm, w_out), (start_hbm, start_ref), (layer_hbm, layer_ref),
    ]
    loads = [pltpu.make_async_copy(a, b, load_sem.at[i]) for i, (a, b) in enumerate(moves)]
    for d in loads:
        d.start()

    s = lax.axis_index("section")
    e = lax.axis_index("expert")
    c = lax.rem(e, 2)
    z = lax.rem(e // 2, 8)
    x = lax.rem(e // 16, 4)
    yh = e // 64
    zh, zl = z // 4, lax.rem(z, 4)

    def at(yy, xx, zz, cc, ss=None):
        return (s if ss is None else ss, ((yy * 4 + xx) * 8 + zz) * 2 + cc)

    def mod(v, n):
        return lax.rem(v + n, n)

    sibling = at(yh, x, z, 1 - c)
    right, left = at(yh, mod(x + 1, 4), z, c), at(yh, mod(x - 1, 4), z, c)
    up, down = at(yh, x, mod(z + 1, 8), c), at(yh, x, mod(z - 1, 8), c)
    me8 = x * 2 + c
    me16 = yh * 8 + x * 2 + zh
    side, odd = zl // 2, lax.rem(zl, 2)
    me_src = (x * 2 + zh) * 2 + side
    role = [(dx, dc) for dx in range(4) for dc in range(2)]

    def role_of(dx, dc):
        xx = mod(x + dx, 4)
        cc = lax.rem(c + dc, 2)
        return xx, cc

    def partner(i, h):
        yy = lax.rem(yh + i // 8, 2)
        xx = mod(x + (i // 2) % 4, 4)
        zz_h, zz_l = (1 - zh, 1 - odd) if i % 2 else (zh, odd)
        return yy * 8 + xx * 2 + zz_h, at(yy, xx, zz_h * 4 + zz_l + 2 * h, c)

    def source(i):
        xx = mod(x - (i // 2) % 4, 4)
        return (xx * 2 + (1 - zh if i % 2 else zh)) * 2

    pending = []

    def copy(src, dst, ssem, rsem, dev):
        return pltpu.make_async_remote_copy(
            src_ref=src, dst_ref=dst, send_sem=ssem, recv_sem=rsem, device_id=dev,
            device_id_type=pl.DeviceIdType.MESH,
        )

    def send(src, dst, ssem, rsem, dev):
        d = copy(src, dst, ssem, rsem, dev)
        d.start()
        pending.append(d)

    def arrived(dst, rsem):
        copy(dst, dst, rsem, rsem, sibling).wait_recv()

    barrier = pltpu.get_barrier_semaphore()
    peers = [at(yh, x, z, c, lax.rem(s + k, 4)) for k in (1, 2, 3)]
    peers += [at(yh, *role_of(dx, dc)[:1], z, role_of(dx, dc)[1]) for dx, dc in role[1:]]
    peers += [up, down]
    peers += [at(1 - yh, x, z, cc) for cc in (0, 1)]
    for dev in peers:
        pl.semaphore_signal(barrier, inc=1, device_id=dev, device_id_type=pl.DeviceIdType.MESH)

    loads[10].wait()
    loads[11].wait()
    start = start_ref[0]
    layer = layer_ref[0]
    loads[0].wait()
    loads[1].wait()

    @pl.when(s == 0)
    def _():
        row = lax.broadcasted_iota(jnp.int32, (128, 128), 0)
        col = lax.broadcasted_iota(jnp.int32, (128, 128), 1)
        turn = (col == row).astype(F32).astype(BF)
        raw[...] = dot(turn, enc_ref[...], NT).astype(BF).reshape(8, CHUNK, width)

    @pl.when(s > 0)
    def _():
        row = lax.broadcasted_iota(jnp.int32, (PATCH, 128), 0)
        col = lax.broadcasted_iota(jnp.int32, (PATCH, 128), 1)
        pick = (col == row + start).astype(F32).astype(BF)
        win[s - 1] = dot(pick, enc_ref[...], NT).astype(BF)

    pl.semaphore_wait(barrier, len(peers))

    for yy in (0, 1):
        here = (yh == yy) & (c == yh)

        @pl.when(here)
        def _(yy=yy):
            pltpu.make_async_copy(w_ref, w0.at[c], self_sem.at[0]).start()

        @pl.when(jnp.logical_not(here))
        def _(yy=yy):
            copy(w_ref, w0.at[c], wx_s.at[yy], wx_r.at[c], at(yy, x, z, yh)).start()

    @pl.when(s == 0)
    def _():
        for k in range(8):
            copy(raw.at[k], raw.at[k], raw_s.at[k], raw_r.at[k], at(yh, x, z, c, 1)).start()

    @pl.when(s > 0)
    def _():
        for k in (1, 2, 3):
            copy(
                win.at[s - 1], win.at[s - 1], win_s.at[k - 1], win_r.at[s - 1],
                at(yh, x, z, c, lax.rem(s + k, 4)),
            ).start()

    loads[2].wait()
    loads[3].wait()
    for i, (dx, dc) in enumerate(role):
        xx, cc = role_of(dx, dc)
        cols = pl.ds(pl.multiple_of((cc * 4 + xx) * 128, 128), 128)
        if i == 0:
            qg[me8] = q_ref[:, cols]
        else:
            send(q_ref.at[:, cols], qg.at[me8], q_s.at[i], q_r.at[i], at(yh, xx, z, cc))

    q_left, q_right, q_far = (mod(x + d, 4) * 2 + c for d in (3, 1, 2))

    def go(src, dst, ssem, rsem, dev):
        copy(src, dst, ssem, rsem, dev).start()

    def patched_chunk(k):
        @pl.when(s > 0)
        def _():
            arrived(raw.at[k], raw_r.at[k])

        @pl.when((s > 0) & (s < 3))
        def _():
            go(raw.at[k], raw.at[k], raw_s.at[k], raw_r.at[k], at(yh, x, z, c, s + 1))

        for i in range(3):
            @pl.when((s != i + 1) & (k == 0))
            def _(i=i):
                arrived(win.at[i], win_r.at[i])

        first = k * CHUNK - start
        row = lax.broadcasted_iota(jnp.int32, (CHUNK, PATCH), 0) + first
        slot = lax.broadcasted_iota(jnp.int32, (CHUNK, PATCH), 1)
        pick = (row == slot).astype(F32).astype(BF)
        window = jnp.where(layer == 1, win[0], jnp.where(layer == 2, win[1], win[2]))
        fresh = dot(pick, window)
        at_row = lax.broadcasted_iota(jnp.int32, fresh.shape, 0) + first
        values = jnp.where((at_row >= 0) & (at_row < PATCH), fresh, raw[k].astype(F32))
        scale = lax.rsqrt(jnp.mean(values * values, axis=-1, keepdims=True) + EPS)
        normed = (values * scale * enc_gain_ref[...]).astype(BF)
        mem[me8, k] = normed
        block = mem.at[me8, k]
        go(block, block, xr_s.at[k], xr_r.at[k], right)
        go(block, block, xl_s.at[k], xl_r.at[k], left)
        go(block, block, sib_s.at[0, k], sib_r.at[0, k], sibling)

    def neighbour_chunk(k):
        block = mem.at[q_left, k]
        arrived(block, xr_r.at[k])

        @pl.when(k < 4)
        def _():
            go(block, block, x2_s.at[k], x2_r.at[k], right)

        go(block, block, sib_s.at[3, k], sib_r.at[3, k], sibling)
        other = mem.at[q_right, k]
        arrived(other, xl_r.at[k])

        @pl.when(k >= 4)
        def _():
            go(other, other, x2_s.at[k], x2_r.at[k], left)

        go(other, other, sib_s.at[1, k], sib_r.at[1, k], sibling)

    def far_chunk(k):
        block = mem.at[q_far, k]
        arrived(block, x2_r.at[k])
        go(block, block, sib_s.at[2, k], sib_r.at[2, k], sibling)

    def ring_up(r, m):
        block = wz.at[m, mod(z - r + 8, 8)]
        go(block, block, zr_s.at[r, m], zr_r.at[r, m], up)

    def ring_down(r, m):
        block = wz.at[m, mod(z + r, 8)]
        go(block, block, zl_s.at[r, m], zl_r.at[r, m], down)

    def from_down(r, m):
        arrived(wz.at[m, mod(z - r + 7, 8)], zr_r.at[r, m])

    def from_up(r, m):
        arrived(wz.at[m, mod(z + r + 1, 8)], zl_r.at[r, m])

    def own_weights():
        for cc in (0, 1):
            here = (c == yh) & (c == cc)

            @pl.when(here)
            def _(cc=cc):
                pltpu.make_async_copy(w_ref, w0.at[cc], self_sem.at[0]).wait()

            @pl.when(jnp.logical_not(here))
            def _(cc=cc):
                arrived(w0.at[cc], wx_r.at[cc])

        for m in range(3):
            both = jnp.concatenate([w0[0, m].astype(F32), w0[1, m].astype(F32)], axis=0)
            wz[m, z] = both.astype(BF)
            ring_up(0, m)
            ring_down(0, m)

    first_a = 2 * s
    first_w = jnp.where(c == yh, 0, jnp.where(s == 0, 8, 5))
    first_z = first_w + 1

    def tick(t, carry):
        k = t - first_a

        @pl.when((k >= 0) & (k < 8))
        def _():
            patched_chunk(k)

        @pl.when(t == first_w)
        def _():
            own_weights()

        kb = k - 3

        @pl.when((kb >= 0) & (kb < 8))
        def _():
            neighbour_chunk(kb)

        for half in (0, 1):
            j = (t - first_z) * 2 + half
            r, m = j // 3, lax.rem(j, 3)

            @pl.when((j >= 0) & (j < 8))
            def _(r=r, m=m):
                from_down(r, m)
                ring_up(r + 1, m)

            @pl.when((j >= 0) & ((j < 6) | (j == 8)))
            def _(r=r, m=m):
                from_up(r, m)
                ring_down(r + 1, m)

        return carry

    lax.fori_loop(0, 18, tick, 0)
    from_down(2, 2), from_down(3, 0), from_down(3, 1)
    from_up(2, 0), from_up(2, 1), from_up(3, 2)
    for i, (dx, dc) in enumerate(role[1:], 1):
        arrived(qg.at[mod(x - dx, 4) * 2 + lax.rem(c + dc, 2)], q_r.at[i])

    first_head = lax.broadcasted_iota(jnp.int32, (16, 128), 1) < HEAD_DIM

    def attend(dx):
        xx = mod(x + dx, 4)
        for k in range(8):
            arrived(mem.at[xx * 2 + (1 - c), k], sib_r.at[dx, k])
        rows = mem[pl.ds(xx * 2, 2)].reshape(256, width)
        kv = dot(rows, wz[0:2].reshape(256, width), NT).astype(BF)
        for cc in (0, 1):
            q = xx * 2 + cc
            keys, values = kv[cc * 128:cc * 128 + 128, :128], kv[cc * 128:cc * 128 + 128, 128:]
            ask = qg[q].astype(F32)
            ask = jnp.concatenate(
                [jnp.where(first_head, ask, 0.0), jnp.where(first_head, 0.0, ask)], axis=0
            )
            exponent = jnp.exp(dot(ask.astype(BF), keys, NT))
            shares = exponent / jnp.sum(exponent, axis=-1, keepdims=True)
            mixed = dot(shares.astype(BF), values)
            context = jnp.where(first_head, mixed[:16], mixed[16:]).astype(BF)
            part[q] = dot(context, wz[2].reshape(128, width)).astype(BF)
        for dc in (0, 1):
            i = dx * 2 + dc
            cc = lax.rem(c + dc, 2)
            if i:
                send(part.at[xx * 2 + cc], pr.at[me8], p_s.at[i], p_r.at[i], at(yh, xx, z, cc))

    attend(0)
    for k in range(4):
        far_chunk(k)
    attend(3)
    for k in range(4, 8):
        far_chunk(k)
    attend(1)
    attend(2)

    row = lax.broadcasted_iota(jnp.int32, (128, 128), 0)
    col = lax.broadcasted_iota(jnp.int32, (128, 128), 1)
    turn = (col == row).astype(F32).astype(BF)
    memory_ref[...] = dot(mem[me8].reshape(128, width), turn, (((0,), (0,)), ((), ()))).astype(BF)
    for d in loads[4:10]:
        d.wait()
    total = dec_ref[...].astype(F32) + part[me8].astype(F32)
    for i, (dx, dc) in enumerate(role[1:], 1):
        q = mod(x - dx, 4) * 2 + lax.rem(c + dc, 2)
        arrived(pr.at[q], p_r.at[i])
        total = total + pr[q].astype(F32)
    residual = total.astype(BF)
    total = residual.astype(F32)
    scale = lax.rsqrt(jnp.mean(total * total, axis=-1, keepdims=True) + EPS)
    normed = (total * scale * ffn_gain_ref[...]).astype(BF)

    row = lax.broadcasted_iota(jnp.int32, (16, 16), 0)
    col = lax.broadcasted_iota(jnp.int32, (16, 16), 1)
    id_row = jnp.broadcast_to(id_ref[...], (16, 16)).astype(F32)
    id_col = jnp.sum(jnp.where(row == col, id_row, 0.0), axis=1, keepdims=True)
    gate = jnp.broadcast_to(gate_ref[...], (16, 16))
    gate = jnp.sum(jnp.where(row == col, gate, 0.0), axis=1, keepdims=True)
    id_row = id_row[0:1]
    same = (jnp.broadcast_to(id_row, (16, 16)) == jnp.broadcast_to(id_col, (16, 16))).astype(F32)
    slot_row = jnp.sum(jnp.where(row < col, same, 0.0), axis=0, keepdims=True)
    slot_col = jnp.sum(jnp.where(col < row, same, 0.0), axis=1, keepdims=True)
    number = lax.broadcasted_iota(jnp.int32, (32, 16), 0)
    chosen = (lax.rem(number, 16).astype(F32) == id_row) & ((number // 16).astype(F32) == slot_row)
    picked = dot(chosen.astype(F32).astype(BF), normed)
    ds[:, 0, :] = picked[:16]
    ds[:, 1, :] = picked[16:]
    dbuf[...] = ds[...].astype(BF)

    far_first = sorted(range(16), key=lambda i: (i // 8, min(i // 2 % 4, 4 - i // 2 % 4) + 2 * (i % 2)))[::-1]

    def exchange(group, block_of, dst, ssem, rsem):
        for i in far_first:
            if i // 8 != group:
                continue
            if i == 0:
                send(
                    block_of(me16, 1 - side), dst.at[0, me_src], ssem.at[0], rsem.at[side],
                    at(yh, x, zh * 4 + lax.rem(zl + 2, 4), c),
                )
            else:
                for h in (0, 1):
                    e16, dev = partner(i, h)
                    send(
                        block_of(e16, h), dst.at[group, me_src],
                        ssem.at[i * 2 + h], rsem.at[i * 2 + side], dev,
                    )

    def exchanged(group, dst, rsem):
        for i in range(group * 8, group * 8 + 8):
            if i == 0:
                arrived(dst.at[0, (x * 2 + zh) * 2 + (1 - side)], rsem.at[1 - side])
            else:
                for h in (0, 1):
                    arrived(dst.at[group, source(i) + h], rsem.at[i * 2 + h])

    across = at(yh, x, zh * 4 + zl + 1 - 2 * odd, c)

    for group in (1, 0):
        exchange(group, lambda e16, h: dbuf.at[e16], d1, d1_s, d1_r)
    d1[0, me_src] = dbuf[me16]

    def share(group):
        exchanged(group, d1, d1_r)
        ds[...] = d1[group].astype(F32)
        g[group, odd, c] = jnp.concatenate([ds[:, 0, :], ds[:, 1, :]], axis=0).astype(BF)
        block = g.at[group, odd, c]
        send(block, block, g_s.at[group], g_r.at[group], across)
        send(block, block, gs_s.at[group, 0], gs_r.at[group, 0], sibling)

    def shared(group):
        block = g.at[group, 1 - odd, c]
        arrived(block, g_r.at[group])
        send(block, block, gs_s.at[group, 1], gs_r.at[group, 1], sibling)

    def work(group):
        for k in (0, 1):
            arrived(g.at[group, odd if k == 0 else 1 - odd, 1 - c], gs_r.at[group, k])
        hidden = jnp.maximum(dot(g[group].reshape(128, width), w_in[...]), 0.0).astype(BF)
        y[group] = dot(hidden, w_out[...], NT).astype(BF).reshape(2, 2, 32, width)
        for k in (0, 1):
            to = lax.rem(odd + 1 + k, 2)
            send(y.at[group, to, 1 - c], rb.at[group, to], rb_s.at[group, k], rb_r.at[group, k], sibling)

    def pair_sum(group):
        arrived(rb.at[group, 1 - odd], rb_r.at[group, 0])
        rt[group] = (y[group, 1 - odd, c].astype(F32) + rb[group, 1 - odd].astype(F32)).astype(BF)
        send(rt.at[group], rz.at[group], rz_s.at[group], rz_r.at[group], across)

    def give_back(group):
        arrived(rb.at[group, odd], rb_r.at[group, 1])
        arrived(rz.at[group], rz_r.at[group])
        total = y[group, odd, c].astype(F32) + rb[group, odd].astype(F32) + rz[group].astype(F32)
        ds[:, 0, :] = total[:16]
        ds[:, 1, :] = total[16:]
        d2[group] = ds[...].astype(BF)
        exchange(group, lambda e16, h: d2.at[group, lax.rem(e16, 8) * 2 + h], ret, d2_s, d2_r)

    share(0), shared(0), share(1), work(0), shared(1), pair_sum(0)
    work(1), pair_sum(1), give_back(1), give_back(0)
    ret[0, me_src] = d2[0, me_src]
    combined = jnp.zeros((16, width), F32)
    number = lax.broadcasted_iota(jnp.int32, (16, 32), 1)
    for group in (0, 1):
        exchanged(group, ret, d2_r)
        ds[...] = ret[group].astype(F32)
        slots = jnp.concatenate([ds[:, 0, :], ds[:, 1, :]], axis=0).astype(BF)
        expert = lax.rem(number, 16) // 2 + 8 * lax.rem(yh + group, 2)
        chosen = (expert.astype(F32) == id_col) & ((number // 16).astype(F32) == slot_col)
        combined = combined + dot(chosen.astype(F32).astype(BF), slots)
    out_ref[...] = (residual.astype(F32) + gate * combined).astype(BF)

    for d in pending:
        d.wait_send()
    for yy in (0, 1):
        @pl.when(jnp.logical_not((yh == yy) & (c == yh)))
        def _(yy=yy):
            copy(w_ref, w0.at[c], wx_s.at[yy], wx_r.at[c], at(yy, x, z, yh)).wait_send()

    @pl.when(s < 3)
    def _():
        for k in range(8):
            copy(raw.at[k], raw.at[k], raw_s.at[k], raw_r.at[k], sibling).wait_send()

    @pl.when(s > 0)
    def _():
        for k in (1, 2, 3):
            copy(
                win.at[s - 1], win.at[s - 1], win_s.at[k - 1], win_r.at[s - 1], sibling
            ).wait_send()

    def sent(ref, sem):
        copy(ref, ref, sem, sem, sibling).wait_send()

    for k in range(8):
        for sem in (xr_s, xl_s, x2_s):
            sent(mem.at[me8, k], sem.at[k])
        for d in range(4):
            sent(mem.at[me8, k], sib_s.at[d, k])
    for r in range(4):
        for m in range(3):
            if r < 3 or m < 2:
                sent(wz.at[m, z], zr_s.at[r, m])
            if r < 3 or m == 2:
                sent(wz.at[m, z], zl_s.at[r, m])


def per_device(
    enc_states, patch_start, patch_layer, enc_gain, dec_states, queries, attn_weight, ffn_gain,
    expert_in, expert_out, expert_id, gate,
):
    rows, width = enc_states.shape[1:]
    hid = expert_in.shape[-1]
    dma = lambda *shape: pltpu.SemaphoreType.DMA(shape)
    vm = lambda *shape: pltpu.VMEM(shape, BF)
    vmem = pl.BlockSpec(memory_space=pltpu.VMEM)
    hbm = pl.BlockSpec(memory_space=pltpu.HBM)
    scratch = [
        pltpu.SMEM((1,), jnp.int32), pltpu.SMEM((1,), jnp.int32),
        vm(width, rows), pltpu.VMEM((1, width), F32), vm(16, width), vm(16, 1024), vm(3, 8, width),
        pltpu.VMEM((1, width), F32), vm(width, hid), vm(width, hid),
        pltpu.VMEM((1, 16), jnp.int32), pltpu.VMEM((1, 16), F32),
        vm(8, 16, width), vm(3, PATCH, width), vm(8, 8, 16, width), vm(2, 3, 8, width),
        vm(3, 8, 16, width), vm(8, 16, 128), vm(8, 16, width), vm(8, 16, width),
        pltpu.VMEM((16, 2, width), F32), vm(16, 2, width), vm(2, 16, 2, width),
        vm(2, 2, 2, 32, width), vm(2, 2, 2, 32, width), vm(2, 2, 32, width), vm(2, 32, width),
        vm(2, 32, width), vm(2, 16, 2, width), vm(2, 16, 2, width),
        dma(12), dma(2), dma(2), dma(8), dma(8), dma(3), dma(3), dma(8), dma(8), dma(1),
        dma(8), dma(8), dma(8), dma(8), dma(8), dma(8), dma(4, 8), dma(4, 8),
        dma(4, 3), dma(4, 3), dma(4, 3), dma(4, 3),
        dma(8), dma(8), dma(32), dma(32), dma(2), dma(2), dma(2, 2), dma(2, 2), dma(2, 2), dma(2, 2),
        dma(2), dma(2), dma(32), dma(32),
    ]
    out, memory = pl.pallas_call(
        kernel,
        out_shape=(
            jax.ShapeDtypeStruct(dec_states.shape[1:], BF),
            jax.ShapeDtypeStruct((width, rows), BF),
        ),
        in_specs=[hbm] * 12,
        out_specs=(vmem, vmem),
        scratch_shapes=scratch,
        compiler_params=pltpu.CompilerParams(
            collective_id=0, has_side_effects=True, vmem_limit_bytes=60 * 1024 * 1024
        ),
    )(
        patch_start, patch_layer, enc_states[0].T, enc_gain, dec_states[0], queries[0],
        jnp.transpose(attn_weight[0], (0, 2, 1)), ffn_gain, expert_in[0, 0], expert_out[0, 0].T,
        expert_id[0].reshape(1, 16), gate,
    )
    return out[None], memory.T


def solution(mesh):
    in_specs = (
        P("section", "expert", None),
        P("expert"),
        P("expert"),
        P(),
        P("section", "expert", None),
        P("section", "expert", None),
        P("section", None, None, "expert"),
        P("section", None),
        P("section", "expert", None, None),
        P("section", "expert", None, None),
        P("section", "expert", None),
        P("section", "expert"),
    )
    out_specs = (P("section", "expert", None), P("expert", None))
    return jax.shard_map(
        per_device, mesh=mesh, in_specs=in_specs, out_specs=out_specs, check_vma=False
    )
```

```python
import jax
import jax.numpy as jnp
from jax import lax
from jax.experimental import pallas as pl
from jax.experimental.pallas import tpu as pltpu
from jax.sharding import PartitionSpec as P

HEAD_DIM = 64
PATCH = 8
CHUNK = 16
EPS = 1e-06
BF, F32 = jnp.bfloat16, jnp.float32
NT = (((1,), (1,)), ((), ()))
NN = (((1,), (0,)), ((), ()))


def dot(a, b, dims=NN):
    return lax.dot_general(a, b, dims, preferred_element_type=F32)


def kernel(
    start_hbm, layer_hbm, enc_hbm, enc_gain_hbm, dec_hbm, q_hbm, w_hbm, ffn_gain_hbm,
    w_in_hbm, w_out_hbm, id_hbm, gate_hbm,
    out_ref, memory_ref,
    start_ref, layer_ref, enc_ref, enc_gain_ref, dec_ref, q_ref, w_ref, ffn_gain_ref, w_in, w_out, id_ref, gate_ref,
    raw, win, mem, w0, wz, qg, part, pr, ds, dbuf, d1, g, y, rb, rz, rt, d2, ret,
    load_sem, wx_s, wx_r, raw_s, raw_r, win_s, win_r, q_s, q_r, self_sem,
    xr_s, xr_r, xl_s, xl_r, x2_s, x2_r, sib_s, sib_r, zr_s, zr_r, zl_s, zl_r,
    p_s, p_r, d1_s, d1_r, g_s, g_r, gs_s, gs_r, rb_s, rb_r, rz_s, rz_r, d2_s, d2_r,
):
    width = enc_ref.shape[0]

    moves = [
        (w_hbm, w_ref), (enc_hbm, enc_ref), (q_hbm, q_ref), (enc_gain_hbm, enc_gain_ref.at[0]),
        (dec_hbm, dec_ref), (ffn_gain_hbm, ffn_gain_ref), (id_hbm, id_ref), (gate_hbm, gate_ref),
        (w_in_hbm, w_in), (w_out_hbm, w_out), (start_hbm, start_ref), (layer_hbm, layer_ref),
    ]
    loads = [pltpu.make_async_copy(a, b, load_sem.at[i]) for i, (a, b) in enumerate(moves)]
    for d in loads:
        d.start()

    s = lax.axis_index("section")
    e = lax.axis_index("expert")
    c = lax.rem(e, 2)
    z = lax.rem(e // 2, 8)
    x = lax.rem(e // 16, 4)
    yh = e // 64
    zh, zl = z // 4, lax.rem(z, 4)

    def at(yy, xx, zz, cc, ss=None):
        return (s if ss is None else ss, ((yy * 4 + xx) * 8 + zz) * 2 + cc)

    def mod(v, n):
        return lax.rem(v + n, n)

    sibling = at(yh, x, z, 1 - c)
    right, left = at(yh, mod(x + 1, 4), z, c), at(yh, mod(x - 1, 4), z, c)
    up, down = at(yh, x, mod(z + 1, 8), c), at(yh, x, mod(z - 1, 8), c)
    me8 = x * 2 + c
    me16 = yh * 8 + x * 2 + zh
    side, odd = zl // 2, lax.rem(zl, 2)
    me_src = (x * 2 + zh) * 2 + side
    role = [(dx, dc) for dx in range(4) for dc in range(2)]

    def role_of(dx, dc):
        xx = mod(x + dx, 4)
        cc = lax.rem(c + dc, 2)
        return xx, cc

    def partner(i, h):
        yy = lax.rem(yh + i // 8, 2)
        xx = mod(x + (i // 2) % 4, 4)
        zz_h, zz_l = (1 - zh, 1 - odd) if i % 2 else (zh, odd)
        return yy * 8 + xx * 2 + zz_h, at(yy, xx, zz_h * 4 + zz_l + 2 * h, c)

    def source(i):
        xx = mod(x - (i // 2) % 4, 4)
        return (xx * 2 + (1 - zh if i % 2 else zh)) * 2

    pending = []

    def copy(src, dst, ssem, rsem, dev):
        return pltpu.make_async_remote_copy(
            src_ref=src, dst_ref=dst, send_sem=ssem, recv_sem=rsem, device_id=dev,
            device_id_type=pl.DeviceIdType.MESH,
        )

    def send(src, dst, ssem, rsem, dev):
        d = copy(src, dst, ssem, rsem, dev)
        d.start()
        pending.append(d)

    def arrived(dst, rsem):
        copy(dst, dst, rsem, rsem, sibling).wait_recv()

    barrier = pltpu.get_barrier_semaphore()
    peers = [at(yh, x, z, c, lax.rem(s + k, 4)) for k in (1, 2, 3)]
    peers += [at(yh, *role_of(dx, dc)[:1], z, role_of(dx, dc)[1]) for dx, dc in role[1:]]
    peers += [up, down]
    peers += [at(1 - yh, x, z, cc) for cc in (0, 1)]
    for dev in peers:
        pl.semaphore_signal(barrier, inc=1, device_id=dev, device_id_type=pl.DeviceIdType.MESH)

    loads[10].wait()
    loads[11].wait()
    start = start_ref[0]
    layer = layer_ref[0]
    loads[0].wait()
    loads[1].wait()

    @pl.when(s == 0)
    def _():
        row = lax.broadcasted_iota(jnp.int32, (128, 128), 0)
        col = lax.broadcasted_iota(jnp.int32, (128, 128), 1)
        turn = (col == row).astype(F32).astype(BF)
        raw[...] = dot(turn, enc_ref[...], NT).astype(BF).reshape(8, CHUNK, width)

    @pl.when(s > 0)
    def _():
        row = lax.broadcasted_iota(jnp.int32, (PATCH, 128), 0)
        col = lax.broadcasted_iota(jnp.int32, (PATCH, 128), 1)
        pick = (col == row + start).astype(F32).astype(BF)
        win[s - 1] = dot(pick, enc_ref[...], NT).astype(BF)

    pl.semaphore_wait(barrier, len(peers))

    for yy in (0, 1):
        here = (yh == yy) & (c == yh)

        @pl.when(here)
        def _(yy=yy):
            pltpu.make_async_copy(w_ref, w0.at[c], self_sem.at[0]).start()

        @pl.when(jnp.logical_not(here))
        def _(yy=yy):
            copy(w_ref, w0.at[c], wx_s.at[yy], wx_r.at[c], at(yy, x, z, yh)).start()

    @pl.when(s == 0)
    def _():
        for k in range(8):
            copy(raw.at[k], raw.at[k], raw_s.at[k], raw_r.at[k], at(yh, x, z, c, 1)).start()

    @pl.when(s > 0)
    def _():
        for k in (1, 2, 3):
            copy(
                win.at[s - 1], win.at[s - 1], win_s.at[k - 1], win_r.at[s - 1],
                at(yh, x, z, c, lax.rem(s + k, 4)),
            ).start()

    loads[2].wait()
    loads[3].wait()
    for i, (dx, dc) in enumerate(role):
        xx, cc = role_of(dx, dc)
        cols = pl.ds(pl.multiple_of((cc * 4 + xx) * 128, 128), 128)
        if i == 0:
            qg[me8] = q_ref[:, cols]
        else:
            send(q_ref.at[:, cols], qg.at[me8], q_s.at[i], q_r.at[i], at(yh, xx, z, cc))

    q_left, q_right, q_far = (mod(x + d, 4) * 2 + c for d in (3, 1, 2))

    def go(src, dst, ssem, rsem, dev):
        copy(src, dst, ssem, rsem, dev).start()

    def patched_chunk(k):
        @pl.when(s > 0)
        def _():
            arrived(raw.at[k], raw_r.at[k])

        @pl.when((s > 0) & (s < 3))
        def _():
            go(raw.at[k], raw.at[k], raw_s.at[k], raw_r.at[k], at(yh, x, z, c, s + 1))

        for i in range(3):
            @pl.when((s != i + 1) & (k == 0))
            def _(i=i):
                arrived(win.at[i], win_r.at[i])

        first = k * CHUNK - start
        row = lax.broadcasted_iota(jnp.int32, (CHUNK, PATCH), 0) + first
        slot = lax.broadcasted_iota(jnp.int32, (CHUNK, PATCH), 1)
        pick = (row == slot).astype(F32).astype(BF)
        window = jnp.where(layer == 1, win[0], jnp.where(layer == 2, win[1], win[2]))
        fresh = dot(pick, window)
        at_row = lax.broadcasted_iota(jnp.int32, fresh.shape, 0) + first
        values = jnp.where((at_row >= 0) & (at_row < PATCH), fresh, raw[k].astype(F32))
        scale = lax.rsqrt(jnp.mean(values * values, axis=-1, keepdims=True) + EPS)
        normed = (values * scale * enc_gain_ref[...]).astype(BF)
        mem[me8, k] = normed
        block = mem.at[me8, k]
        go(block, block, xr_s.at[k], xr_r.at[k], right)
        go(block, block, xl_s.at[k], xl_r.at[k], left)
        go(block, block, sib_s.at[0, k], sib_r.at[0, k], sibling)

    def neighbour_chunk(k):
        block = mem.at[q_left, k]
        arrived(block, xr_r.at[k])

        @pl.when(k < 4)
        def _():
            go(block, block, x2_s.at[k], x2_r.at[k], right)

        go(block, block, sib_s.at[3, k], sib_r.at[3, k], sibling)
        other = mem.at[q_right, k]
        arrived(other, xl_r.at[k])

        @pl.when(k >= 4)
        def _():
            go(other, other, x2_s.at[k], x2_r.at[k], left)

        go(other, other, sib_s.at[1, k], sib_r.at[1, k], sibling)

    def far_chunk(k):
        block = mem.at[q_far, k]
        arrived(block, x2_r.at[k])
        go(block, block, sib_s.at[2, k], sib_r.at[2, k], sibling)

    def ring_up(r, m):
        block = wz.at[m, mod(z - r + 8, 8)]
        go(block, block, zr_s.at[r, m], zr_r.at[r, m], up)

    def ring_down(r, m):
        block = wz.at[m, mod(z + r, 8)]
        go(block, block, zl_s.at[r, m], zl_r.at[r, m], down)

    def from_down(r, m):
        arrived(wz.at[m, mod(z - r + 7, 8)], zr_r.at[r, m])

    def from_up(r, m):
        arrived(wz.at[m, mod(z + r + 1, 8)], zl_r.at[r, m])

    def own_weights():
        for cc in (0, 1):
            here = (c == yh) & (c == cc)

            @pl.when(here)
            def _(cc=cc):
                pltpu.make_async_copy(w_ref, w0.at[cc], self_sem.at[0]).wait()

            @pl.when(jnp.logical_not(here))
            def _(cc=cc):
                arrived(w0.at[cc], wx_r.at[cc])

        for m in range(3):
            both = jnp.concatenate([w0[0, m].astype(F32), w0[1, m].astype(F32)], axis=0)
            wz[m, z] = both.astype(BF)
            ring_up(0, m)
            ring_down(0, m)

    first_a = 2 * s
    first_w = jnp.where(c == yh, 0, jnp.where(s == 0, 8, 5))
    first_z = first_w + 1

    def tick(t, carry):
        k = t - first_a

        @pl.when((k >= 0) & (k < 8))
        def _():
            patched_chunk(k)

        @pl.when(t == first_w)
        def _():
            own_weights()

        kb = k - 4

        @pl.when((kb >= 0) & (kb < 8))
        def _():
            neighbour_chunk(kb)

        for half in (0, 1):
            j = (t - first_z) * 2 + half
            r, m = j // 3, lax.rem(j, 3)

            @pl.when((j >= 0) & (j < 8))
            def _(r=r, m=m):
                from_down(r, m)
                ring_up(r + 1, m)

            @pl.when((j >= 0) & ((j < 6) | (j == 8)))
            def _(r=r, m=m):
                from_up(r, m)
                ring_down(r + 1, m)

        return carry

    lax.fori_loop(0, 19, tick, 0)
    from_down(2, 2), from_down(3, 0), from_down(3, 1)
    from_up(2, 0), from_up(2, 1), from_up(3, 2)
    for i, (dx, dc) in enumerate(role[1:], 1):
        arrived(qg.at[mod(x - dx, 4) * 2 + lax.rem(c + dc, 2)], q_r.at[i])

    first_head = lax.broadcasted_iota(jnp.int32, (16, 128), 1) < HEAD_DIM

    def attend(dx):
        xx = mod(x + dx, 4)
        for k in range(8):
            arrived(mem.at[xx * 2 + (1 - c), k], sib_r.at[dx, k])
        rows = mem[pl.ds(xx * 2, 2)].reshape(256, width)
        kv = dot(rows, wz[0:2].reshape(256, width), NT).astype(BF)
        for cc in (0, 1):
            q = xx * 2 + cc
            keys, values = kv[cc * 128:cc * 128 + 128, :128], kv[cc * 128:cc * 128 + 128, 128:]
            ask = qg[q].astype(F32)
            ask = jnp.concatenate(
                [jnp.where(first_head, ask, 0.0), jnp.where(first_head, 0.0, ask)], axis=0
            )
            exponent = jnp.exp(dot(ask.astype(BF), keys, NT))
            shares = exponent / jnp.sum(exponent, axis=-1, keepdims=True)
            mixed = dot(shares.astype(BF), values)
            context = jnp.where(first_head, mixed[:16], mixed[16:]).astype(BF)
            part[q] = dot(context, wz[2].reshape(128, width)).astype(BF)
        for dc in (0, 1):
            i = dx * 2 + dc
            cc = lax.rem(c + dc, 2)
            if i:
                send(part.at[xx * 2 + cc], pr.at[me8], p_s.at[i], p_r.at[i], at(yh, xx, z, cc))

    attend(0)
    for k in range(4):
        far_chunk(k)
    attend(3)
    for k in range(4, 8):
        far_chunk(k)
    attend(1)
    attend(2)

    row = lax.broadcasted_iota(jnp.int32, (128, 128), 0)
    col = lax.broadcasted_iota(jnp.int32, (128, 128), 1)
    turn = (col == row).astype(F32).astype(BF)
    memory_ref[...] = dot(mem[me8].reshape(128, width), turn, (((0,), (0,)), ((), ()))).astype(BF)
    for d in loads[4:10]:
        d.wait()
    total = dec_ref[...].astype(F32) + part[me8].astype(F32)
    for i, (dx, dc) in enumerate(role[1:], 1):
        q = mod(x - dx, 4) * 2 + lax.rem(c + dc, 2)
        arrived(pr.at[q], p_r.at[i])
        total = total + pr[q].astype(F32)
    residual = total.astype(BF)
    total = residual.astype(F32)
    scale = lax.rsqrt(jnp.mean(total * total, axis=-1, keepdims=True) + EPS)
    normed = (total * scale * ffn_gain_ref[...]).astype(BF)

    row = lax.broadcasted_iota(jnp.int32, (16, 16), 0)
    col = lax.broadcasted_iota(jnp.int32, (16, 16), 1)
    id_row = jnp.broadcast_to(id_ref[...], (16, 16)).astype(F32)
    id_col = jnp.sum(jnp.where(row == col, id_row, 0.0), axis=1, keepdims=True)
    gate = jnp.broadcast_to(gate_ref[...], (16, 16))
    gate = jnp.sum(jnp.where(row == col, gate, 0.0), axis=1, keepdims=True)
    id_row = id_row[0:1]
    same = (jnp.broadcast_to(id_row, (16, 16)) == jnp.broadcast_to(id_col, (16, 16))).astype(F32)
    slot_row = jnp.sum(jnp.where(row < col, same, 0.0), axis=0, keepdims=True)
    slot_col = jnp.sum(jnp.where(col < row, same, 0.0), axis=1, keepdims=True)
    number = lax.broadcasted_iota(jnp.int32, (32, 16), 0)
    chosen = (lax.rem(number, 16).astype(F32) == id_row) & ((number // 16).astype(F32) == slot_row)
    picked = dot(chosen.astype(F32).astype(BF), normed)
    ds[:, 0, :] = picked[:16]
    ds[:, 1, :] = picked[16:]
    dbuf[...] = ds[...].astype(BF)

    far_first = sorted(range(16), key=lambda i: (i // 8, min(i // 2 % 4, 4 - i // 2 % 4) + 2 * (i % 2)))[::-1]

    def exchange(group, block_of, dst, ssem, rsem):
        for i in far_first:
            if i // 8 != group:
                continue
            if i == 0:
                send(
                    block_of(me16, 1 - side), dst.at[0, me_src], ssem.at[0], rsem.at[side],
                    at(yh, x, zh * 4 + lax.rem(zl + 2, 4), c),
                )
            else:
                for h in (0, 1):
                    e16, dev = partner(i, h)
                    send(
                        block_of(e16, h), dst.at[group, me_src],
                        ssem.at[i * 2 + h], rsem.at[i * 2 + side], dev,
                    )

    def exchanged(group, dst, rsem):
        for i in range(group * 8, group * 8 + 8):
            if i == 0:
                arrived(dst.at[0, (x * 2 + zh) * 2 + (1 - side)], rsem.at[1 - side])
            else:
                for h in (0, 1):
                    arrived(dst.at[group, source(i) + h], rsem.at[i * 2 + h])

    across = at(yh, x, zh * 4 + zl + 1 - 2 * odd, c)

    for group in (1, 0):
        exchange(group, lambda e16, h: dbuf.at[e16], d1, d1_s, d1_r)
    d1[0, me_src] = dbuf[me16]

    def share(group):
        exchanged(group, d1, d1_r)
        ds[...] = d1[group].astype(F32)
        g[group, odd, c] = jnp.concatenate([ds[:, 0, :], ds[:, 1, :]], axis=0).astype(BF)
        block = g.at[group, odd, c]
        send(block, block, g_s.at[group], g_r.at[group], across)
        send(block, block, gs_s.at[group, 0], gs_r.at[group, 0], sibling)

    def shared(group):
        block = g.at[group, 1 - odd, c]
        arrived(block, g_r.at[group])
        send(block, block, gs_s.at[group, 1], gs_r.at[group, 1], sibling)

    def work(group):
        for k in (0, 1):
            arrived(g.at[group, odd if k == 0 else 1 - odd, 1 - c], gs_r.at[group, k])
        hidden = jnp.maximum(dot(g[group].reshape(128, width), w_in[...]), 0.0).astype(BF)
        y[group] = dot(hidden, w_out[...], NT).astype(BF).reshape(2, 2, 32, width)
        for k in (0, 1):
            to = lax.rem(odd + 1 + k, 2)
            send(y.at[group, to, 1 - c], rb.at[group, to], rb_s.at[group, k], rb_r.at[group, k], sibling)

    def pair_sum(group):
        arrived(rb.at[group, 1 - odd], rb_r.at[group, 0])
        rt[group] = (y[group, 1 - odd, c].astype(F32) + rb[group, 1 - odd].astype(F32)).astype(BF)
        send(rt.at[group], rz.at[group], rz_s.at[group], rz_r.at[group], across)

    def give_back(group):
        arrived(rb.at[group, odd], rb_r.at[group, 1])
        arrived(rz.at[group], rz_r.at[group])
        total = y[group, odd, c].astype(F32) + rb[group, odd].astype(F32) + rz[group].astype(F32)
        ds[:, 0, :] = total[:16]
        ds[:, 1, :] = total[16:]
        d2[group] = ds[...].astype(BF)
        exchange(group, lambda e16, h: d2.at[group, lax.rem(e16, 8) * 2 + h], ret, d2_s, d2_r)

    share(0), shared(0), share(1), work(0), shared(1), pair_sum(0)
    work(1), pair_sum(1), give_back(1), give_back(0)
    ret[0, me_src] = d2[0, me_src]
    combined = jnp.zeros((16, width), F32)
    number = lax.broadcasted_iota(jnp.int32, (16, 32), 1)
    for group in (0, 1):
        exchanged(group, ret, d2_r)
        ds[...] = ret[group].astype(F32)
        slots = jnp.concatenate([ds[:, 0, :], ds[:, 1, :]], axis=0).astype(BF)
        expert = lax.rem(number, 16) // 2 + 8 * lax.rem(yh + group, 2)
        chosen = (expert.astype(F32) == id_col) & ((number // 16).astype(F32) == slot_col)
        combined = combined + dot(chosen.astype(F32).astype(BF), slots)
    out_ref[...] = (residual.astype(F32) + gate * combined).astype(BF)

    for d in pending:
        d.wait_send()
    for yy in (0, 1):
        @pl.when(jnp.logical_not((yh == yy) & (c == yh)))
        def _(yy=yy):
            copy(w_ref, w0.at[c], wx_s.at[yy], wx_r.at[c], at(yy, x, z, yh)).wait_send()

    @pl.when(s < 3)
    def _():
        for k in range(8):
            copy(raw.at[k], raw.at[k], raw_s.at[k], raw_r.at[k], sibling).wait_send()

    @pl.when(s > 0)
    def _():
        for k in (1, 2, 3):
            copy(
                win.at[s - 1], win.at[s - 1], win_s.at[k - 1], win_r.at[s - 1], sibling
            ).wait_send()

    def sent(ref, sem):
        copy(ref, ref, sem, sem, sibling).wait_send()

    for k in range(8):
        for sem in (xr_s, xl_s, x2_s):
            sent(mem.at[me8, k], sem.at[k])
        for d in range(4):
            sent(mem.at[me8, k], sib_s.at[d, k])
    for r in range(4):
        for m in range(3):
            if r < 3 or m < 2:
                sent(wz.at[m, z], zr_s.at[r, m])
            if r < 3 or m == 2:
                sent(wz.at[m, z], zl_s.at[r, m])


def per_device(
    enc_states, patch_start, patch_layer, enc_gain, dec_states, queries, attn_weight, ffn_gain,
    expert_in, expert_out, expert_id, gate,
):
    rows, width = enc_states.shape[1:]
    hid = expert_in.shape[-1]
    dma = lambda *shape: pltpu.SemaphoreType.DMA(shape)
    vm = lambda *shape: pltpu.VMEM(shape, BF)
    vmem = pl.BlockSpec(memory_space=pltpu.VMEM)
    hbm = pl.BlockSpec(memory_space=pltpu.HBM)
    scratch = [
        pltpu.SMEM((1,), jnp.int32), pltpu.SMEM((1,), jnp.int32),
        vm(width, rows), pltpu.VMEM((1, width), F32), vm(16, width), vm(16, 1024), vm(3, 8, width),
        pltpu.VMEM((1, width), F32), vm(width, hid), vm(width, hid),
        pltpu.VMEM((1, 16), jnp.int32), pltpu.VMEM((1, 16), F32),
        vm(8, 16, width), vm(3, PATCH, width), vm(8, 8, 16, width), vm(2, 3, 8, width),
        vm(3, 8, 16, width), vm(8, 16, 128), vm(8, 16, width), vm(8, 16, width),
        pltpu.VMEM((16, 2, width), F32), vm(16, 2, width), vm(2, 16, 2, width),
        vm(2, 2, 2, 32, width), vm(2, 2, 2, 32, width), vm(2, 2, 32, width), vm(2, 32, width),
        vm(2, 32, width), vm(2, 16, 2, width), vm(2, 16, 2, width),
        dma(12), dma(2), dma(2), dma(8), dma(8), dma(3), dma(3), dma(8), dma(8), dma(1),
        dma(8), dma(8), dma(8), dma(8), dma(8), dma(8), dma(4, 8), dma(4, 8),
        dma(4, 3), dma(4, 3), dma(4, 3), dma(4, 3),
        dma(8), dma(8), dma(32), dma(32), dma(2), dma(2), dma(2, 2), dma(2, 2), dma(2, 2), dma(2, 2),
        dma(2), dma(2), dma(32), dma(32),
    ]
    out, memory = pl.pallas_call(
        kernel,
        out_shape=(
            jax.ShapeDtypeStruct(dec_states.shape[1:], BF),
            jax.ShapeDtypeStruct((width, rows), BF),
        ),
        in_specs=[hbm] * 12,
        out_specs=(vmem, vmem),
        scratch_shapes=scratch,
        compiler_params=pltpu.CompilerParams(
            collective_id=0, has_side_effects=True, vmem_limit_bytes=60 * 1024 * 1024
        ),
    )(
        patch_start, patch_layer, enc_states[0].T, enc_gain, dec_states[0], queries[0],
        jnp.transpose(attn_weight[0], (0, 2, 1)), ffn_gain, expert_in[0, 0], expert_out[0, 0].T,
        expert_id[0].reshape(1, 16), gate,
    )
    return out[None], memory.T


def solution(mesh):
    in_specs = (
        P("section", "expert", None),
        P("expert"),
        P("expert"),
        P(),
        P("section", "expert", None),
        P("section", "expert", None),
        P("section", None, None, "expert"),
        P("section", None),
        P("section", "expert", None, None),
        P("section", "expert", None, None),
        P("section", "expert", None),
        P("section", "expert"),
    )
    out_specs = (P("section", "expert", None), P("expert", None))
    return jax.shard_map(
        per_device, mesh=mesh, in_specs=in_specs, out_specs=out_specs, check_vma=False
    )
```
